256 devices in a mesh: val: 4 (over z_hi), cond: 64 (over y, z_lo, x, core).
Axes of the slice: x: 4, y: 4, z: 8 (z_hi: 4, z_lo: 2; z = z_hi * 2 + z_lo), core: 2. Of those that a mesh axis runs over, the one named last changes fastest.
Arguments:
- val_orbitals: bfloat16 [4, 262144], P('val', 'cond'), may hold values from -6 to 6
- cond_orbitals: bfloat16 [64, 262144], P('cond', 'val'), may hold values from -6 to 6
- val_energy: float32 [4], P('val'), may hold values from -3 to -0.2
- cond_energy: float32 [64], P('cond'), may hold values from 0.5 to 5
- plane_index: int32 [19968], replicated, may hold values from 0 to 262143, as said below
- column_index: int32 [2048], replicated, may hold values from 0 to 19967, as said below
Outputs:
- chi_block: float32 [19968, 2048], P('cond', 'val')
The draws below stay inside these ranges and needn't reach their ends.
Inputs may be any that keep to these rules, and one draw needn't show every extreme that they name: `plane_index`: distinct grid indices; 0 and 262143 are always among them. `column_index`: distinct plane-wave indices; 0 and 19967 are always among them.
All inputs are finite; a program needn't handle non-finite values.
Results may differ from the reference program's by a relative error of at most 0.014.
Values may be sent and summed in bfloat16 or wider, within the bound.
A program may use at most 64 MiB of HBM per device.

```python
import math
import jax
import jax.numpy as jnp
from jax import lax

NFFT = 64
NG = 19968
NCOL = 2048
NV = 4
NC = 64
GRID = 262144


def distinct_indices(key, total, count):
    first, second = jax.random.split(key)
    inner = jax.random.permutation(first, total - 2)[:count - 2] + 1
    joined = jnp.concatenate([jnp.array([0, total - 1], jnp.int32), inner.astype(jnp.int32)])
    return jax.random.permutation(second, joined).astype(jnp.int32)


def draw_plane_index(key, part):
    key = jax.random.fold_in(key, 11)
    return distinct_indices(key, GRID, NG)


def draw_column_index(key, part):
    key = jax.random.fold_in(key, 23)
    return distinct_indices(key, NG, NCOL)


def block_levels(rng, dims, shards, low, largest):
    factor_of, own = 1.0, jax.random.fold_in(rng, 6)
    for axis_at, shards_of in shards:
        steps = jnp.exp(jax.random.uniform(jax.random.fold_in(own, axis_at), (shards_of,), jnp.float32, low / len(shards), largest / len(shards)))
        factor_of = factor_of * jnp.repeat(steps, dims[axis_at] // shards_of).reshape([-1 if axis == axis_at else 1 for axis in range(len(dims))])
    return factor_of


def gaussian(own_key, shape, width, reach, shards=(), held_as=jnp.bfloat16):
    entries = width * jax.random.normal(own_key, shape, jnp.float32)
    if shards:
        entries = entries * block_levels(own_key, shape, shards, -0.22, 0.18)
    return jnp.clip(entries, -reach, reach).astype(held_as)


def setup_inputs(seed: int = 0) -> dict:
    streams_of = jax.random.split(jax.random.key(seed), 7)
    val_orbitals = gaussian(streams_of[0], (NV, GRID), 1.0, 6.0, ((0, 4), (1, 64)))
    cond_orbitals = gaussian(streams_of[1], (NC, GRID), 1.0, 6.0, ((0, 64), (1, 4)))
    val_energy = jnp.clip(-3.0 + 2.8 * jax.random.uniform(streams_of[2], (NV,), jnp.float32) ** block_levels(streams_of[2], (NV,), ((0, 4),), -0.2, 0.2), -3.0, -0.2)
    cond_energy = jnp.clip(0.5 + 4.5 * jax.random.uniform(streams_of[3], (NC,), jnp.float32) ** block_levels(streams_of[3], (NC,), ((0, 64),), -0.2, 0.2), 0.5, 5.0)
    plane_index = draw_plane_index(jax.random.fold_in(streams_of[6], 71), 0)
    column_index = draw_column_index(jax.random.fold_in(streams_of[6], 71), 0)
    return dict(val_orbitals=val_orbitals, cond_orbitals=cond_orbitals, val_energy=val_energy, cond_energy=cond_energy, plane_index=plane_index, column_index=column_index)


def reference(val_orbitals, cond_orbitals, val_energy, cond_energy, plane_index, column_index):
    cond_wide = cond_orbitals.astype(jnp.float32)

    def one_band(packed):
        orbital, energy = packed
        density = orbital.astype(jnp.float32)[None, :] * cond_wide
        spectrum = jnp.fft.fftn(density.reshape(NC, NFFT, NFFT, NFFT), axes=(1, 2, 3)).reshape(NC, GRID)
        picked = spectrum[:, plane_index]
        factor = jnp.sqrt(1.0 / ((cond_energy - energy) * math.sqrt(NV * NC) * GRID))
        real_part = (jnp.real(picked) * factor[:, None]).astype(jnp.bfloat16)
        imag_part = (jnp.imag(picked) * factor[:, None]).astype(jnp.bfloat16)
        return jnp.stack([real_part, imag_part], 0)
    pair_values = lax.map(one_band, (val_orbitals, val_energy))
    pair_values = pair_values.reshape(NV * 2 * NC, NG)
    columns = pair_values[:, column_index]
    return -jnp.dot(pair_values.T, columns, preferred_element_type=jnp.float32)
```

```python
import math

import jax
import jax.numpy as jnp
import ml_dtypes
import numpy as np
from jax import lax
from jax.experimental import pallas as pl
from jax.experimental.pallas import tpu as pltpu
from jax.sharding import PartitionSpec as P

N = 64
GRID = N**3
BF = jnp.bfloat16
F32 = jnp.float32
ROWS = 312


def split(a):
    hi = a.astype(ml_dtypes.bfloat16)
    return hi, (a - hi.astype(np.float64)).astype(ml_dtypes.bfloat16)


def tables():
    k = np.arange(N)
    ang = 2 * np.pi * (k[:, None] * k[None, :] % N) / N
    cos, sin = np.cos(ang), np.sin(ang)
    tz = np.zeros((2, N, 2, 2, N))
    for par in range(2):
        tz[par, :, 0, par, :] = cos
        tz[par, :, 1, par, :] = -sin
    tz = tz.reshape(128, 256)
    tz = np.concatenate([tz, tz], 0).astype(ml_dtypes.bfloat16)
    h = np.arange(32)
    ang = 2 * np.pi * (h[:, None] * h[None, :] % 32) / 32
    ty = np.block([[np.cos(ang), np.sin(ang)], [-np.sin(ang), np.cos(ang)]])
    hi, lo = split(ty)
    ty = np.concatenate([hi, lo, hi], 1)
    tx = np.zeros((80, 128))
    tx[:32, :64], tx[:32, 64:] = cos[:32], sin[:32]
    tx[32:64, :64], tx[32:64, 64:] = -sin[:32], cos[:32]
    tx[64, :64] = cos[32]
    tx[65, 64:] = cos[32]
    tx = np.concatenate([tx, tx], 1).astype(ml_dtypes.bfloat16)
    tw = np.zeros((2, 32, 128), np.float32)
    tw[0, :, :64] = 1.0
    ang = 2 * np.pi * h / N
    tw[0, :, 64:] = np.cos(ang)[:, None]
    tw[1, :, 64:] = -np.sin(ang)[:, None]
    return tz, ty, tx, tw


def cond_id(s, xy):
    return (xy // 4) * 16 + (s // 2) * 8 + (xy % 4) * 2 + s % 2


def lanes(shape):
    return lax.broadcasted_iota(jnp.int32, shape, len(shape) - 1)


def subl(shape):
    return lax.broadcasted_iota(jnp.int32, shape, len(shape) - 2)


def order_planes(plane_ref, ix_ref):
    lane = lanes((3, 128))

    def take(start):
        row, off = start // 128, start % 128
        a = plane_ref[row : row + 3, :]
        if off:
            if row + 4 <= 156:
                b = plane_ref[row + 1 : row + 4, :]
            else:
                b = jnp.concatenate([plane_ref[row + 1 : row + 3, :], a[2:3]], 0)
            a = jnp.where(lane < 128 - off, pltpu.roll(a, 128 - off, 1), pltpu.roll(b, 128 - off, 1))
        return a

    for s in range(4):
        for m in range(8):
            even = take(ROWS * cond_id(s, 2 * m))
            odd = take(ROWS * cond_id(s, 2 * m + 1) - 64)
            at = 16 + s * 40 + m * 5
            ix_ref[at : at + 2, :] = even[:2]
            ix_ref[at + 2 : at + 3, :] = jnp.where(lane[:1] < 64, even[2:], odd[:1])
            ix_ref[at + 3 : at + 5, :] = odd[1:]


def compose_columns(plane_ref, col_ref, ix_ref):
    plane = jnp.concatenate([plane_ref[...], jnp.zeros((100, 128), jnp.int32)], 0)
    digits = [
        jnp.transpose(((plane >> sh) & 63).astype(F32), (1, 0)).astype(BF) for sh in (12, 6, 0)
    ]
    left = jnp.concatenate(digits, 0)

    def tile(t, carry):
        col = jnp.concatenate([col_ref[pl.ds(2 * t, 1), :], col_ref[pl.ds(2 * t + 1, 1), :]], 1)
        hot = jnp.where(subl((256, 256)) == (col >> 7), 1.0, 0.0).astype(BF)
        prod = jnp.dot(left, hot, preferred_element_type=F32)
        mask = subl((128, 256)) == (col & 127)
        kx, ky, kz = [
            jnp.sum(jnp.where(mask, prod[128 * d : 128 * d + 128], 0.0), axis=0, keepdims=True)
            for d in range(3)
        ]
        flat = (kx * 4096.0 + ky * 64.0 + kz).astype(jnp.int32)
        ix_ref[pl.ds(2 * t, 1), :] = flat[:, :128]
        ix_ref[pl.ds(2 * t + 1, 1), :] = flat[:, 128:]
        return carry

    lax.fori_loop(0, 8, tile, 0, unroll=4)


def fold_indices(ix_ref, fx_ref):
    n = ix_ref[...]
    kx, ky, kz = n >> 12, (n >> 6) & 63, n & 63
    low = (kx & 31) == 0
    yline = (ky & 31) == 0
    zpoint = (kz & 31) == 0
    neg = kx > 32
    neg = neg | (low & ~yline & ((kx == 0) == (ky > 32)))
    neg = neg | (low & yline & ~zpoint & ((ky == 0) == (kz > 32)))
    special = low & yline & zpoint & ((ky == 0) == (kz == 32))
    turn = lambda k: jnp.where(neg, (64 - k) & 63, k)
    kx, ky, kz = turn(kx), turn(ky), turn(kz)
    slot_y = jnp.where(low & yline, kx, ky)
    fx_ref[0] = (kx & 31).astype(F32)
    fx_ref[1] = jnp.where(special, 99, slot_y & 15).astype(F32)
    line = ((slot_y >> 4) & 1) * 128 + (slot_y >> 5) * 64 + kz
    fx_ref[2] = (line & 15).astype(F32)
    fx_ref[5] = (line >> 4).astype(F32)
    fx_ref[3] = jnp.where(neg, -1.0, 1.0)
    fx_ref[4] = jnp.where(special, (kx >> 5) * 2 + (ky >> 5), 9).astype(F32)


def transform(ready, vf, cf, tz, ty, tw, bs):
    low = lanes((32, 128)) < 64

    def planes(n, carry):
        for y, zl in ready(n):
            a = vf[y, zl].reshape(256, 128).astype(F32)
            b = cf[y, pl.ds(pl.multiple_of(zl * 256, 256), 256), :].astype(F32)
            d = a * b
            hi = d.astype(BF)
            lo = (d - hi.astype(F32)).astype(BF)
            az = jnp.dot(jnp.concatenate([hi, lo], 1), tz[...], preferred_element_type=F32)
            for m in range(4):
                cols = []
                for x in (2 * m, 2 * m + 1):
                    blk = az[x * 32 : x * 32 + 32]
                    cols.append(jnp.concatenate([blk[:, :128], blk[:, 128:]], 0))
                r = jnp.concatenate(cols, 1)
                hi = r.astype(BF)
                lo = (r - hi.astype(F32)).astype(BF)
                g = jnp.dot(ty[...], jnp.concatenate([hi, hi, lo], 0), preferred_element_type=F32)
                for e in range(2):
                    gr, gi = g[:32, e * 128 : e * 128 + 128], g[32:, e * 128 : e * 128 + 128]
                    yr = gr * tw[0] - gi * tw[1]
                    yi = gr * tw[1] + gi * tw[0]
                    at = (y * 16 + zl * 8 + 2 * m + e) * 32
                    for part, v in ((0, yr), (1, yi)):
                        rv = pltpu.roll(v, 64, 1)
                        out = jnp.where(low, rv + v, rv - v)
                        bs[pl.ds(pl.multiple_of(part * 2048 + at, 32), 32), :] = out
        return carry

    lax.fori_loop(0, 4, planes, 0)


def lines_of(fac_ref, tx, bs, wt, sp):
    fac = fac_ref[0:1, :]

    def lines(i, carry):
        b = [bs[pl.ds(4 * i + j, 128, stride=32), :] for j in range(4)]
        r = jnp.concatenate(b, 1)
        hi = r.astype(BF)
        lo = (r - hi.astype(F32)).astype(BF)
        f = jnp.dot(tx[...], jnp.concatenate([hi, lo], 0), preferred_element_type=F32)
        lane = lanes((1, 128))
        top = subl((32, 128)) == 0
        for part in range(2):
            blocks = []
            for j in range(4):
                main = f[32 * part : 32 * part + 32, 128 * j : 128 * j + 128] * fac
                edge = f[64 + part : 65 + part, 128 * j : 128 * j + 128] * fac
                row = main[0:1]
                new = jnp.where(lane < 64, row, edge)
                if j == 0:
                    first = jnp.where(
                        lane < 32,
                        row,
                        jnp.where(
                            lane < 64,
                            pltpu.roll(row, 64, 1),
                            jnp.where(lane < 96, pltpu.roll(edge, 64, 1), edge),
                        ),
                    )
                    if part == 0:

                        @pl.when(i == 0)
                        def _():
                            for n, (v, at) in enumerate(
                                ((row, 32), (row, 64), (edge, 32), (edge, 64))
                            ):
                                pick = jnp.sum(
                                    jnp.where(lane == at, v, 0.0), axis=1, keepdims=True
                                )
                                pick = pick.astype(BF).astype(F32)
                                sp[n : n + 1, :] = jnp.broadcast_to(pick, (1, 256))

                    new = jnp.where(i == 0, first, new)
                blocks.append(jnp.where(top, jnp.broadcast_to(new, (32, 128)), main))
            whole = jnp.transpose(jnp.concatenate(blocks, 0), (1, 0)).astype(BF)
            rows = pl.ds(pl.multiple_of(256 * part + (i // 4) * 128, 128), 128)
            wt[rows, pl.ds(pl.multiple_of((i % 4) * 128, 128), 128)] = whole
        return carry

    lax.fori_loop(0, 8, lines, 0, unroll=2)


def pick_tile(t, fx, wt, sp):
    def row(n):
        return jnp.concatenate([fx[n, pl.ds(2 * t, 1), :], fx[n, pl.ds(2 * t + 1, 1), :]], 1)

    kx = jnp.broadcast_to(row(0), (32, 256)).astype(BF)
    ky = jnp.broadcast_to(row(1), (16, 256)).astype(BF)
    index = subl((32, 256)).astype(F32).astype(BF)
    one, zero = jnp.ones((32, 256), BF), jnp.zeros((16, 256), BF)
    base = jnp.where(kx == index, one, jnp.zeros((32, 256), BF))
    hot = []
    for j in range(16):
        here = ky == jnp.asarray(j, BF)
        hot += [jnp.where(here, base[:16], zero), jnp.where(here, base[16:], zero)]
    hot = jnp.concatenate(hot, 0)
    prod = jnp.dot(wt[...], hot, preferred_element_type=F32).astype(BF)
    high = jnp.broadcast_to(row(5), (16, 256)).astype(BF)
    chosen = [prod[:16], prod[256:272]]
    for n in range(1, 16):
        here = high == jnp.asarray(n, BF)
        for part in range(2):
            at = 256 * part + 16 * n
            chosen[part] = jnp.where(here, prod[at : at + 16], chosen[part])
    line = subl((16, 256)).astype(F32) == row(2)
    re, im = [
        jnp.sum(jnp.where(line, v.astype(F32), 0.0), axis=0, keepdims=True) for v in chosen
    ]
    kind = row(4)
    for n in range(4):
        re = jnp.where(kind == float(n), sp[n : n + 1, :], re)
    return re, im * row(3)


def kernel(
    val_in, cond_ref, ve_ref, ce_ref, plane_ref, col_ref, tz, ty, tx, tw,
    rx, cx,
    val_ref, wide, vf, cf, facs, fac, ix, fx, bs, wt, sp, pv, cb, zs, rz, rf, xs,
    s_val, r_val, s_cond, r_cond, s_pass, s_sib, r_sib, s_fac, r_fac,
    s_vf, r_va, r_vb, r_vy, r_vx,
    s_cb, r_cb, s_cx, r_cx, s_cs, r_cs, s_rz, r_rz, r_rw, s_rx, r_rx,
):
    p = lax.axis_index("val")
    c = lax.axis_index("cond")
    y, zl, x, core = c // 16, (c // 8) % 2, (c // 2) % 4, c % 2
    s = zl * 2 + core
    xy = y * 4 + x
    me = s * 4 + p
    base = y * 16 + x * 2
    at_s = lambda n: base + (n >> 1) * 8 + (n & 1)
    by_s = lambda k: c ^ (((k >> 1) << 3) | (k & 1))
    by_xy = lambda k: c ^ (((k >> 2) << 4) | ((k & 3) << 1))
    twin = p == s
    cond_of = lambda o: (c & 9) | ((o >> 2) << 4) | ((o & 3) << 1)

    def remote(src, dst, send, recv, dp, dc):
        return pltpu.make_async_remote_copy(
            src_ref=src, dst_ref=dst, send_sem=send, recv_sem=recv,
            device_id=(dp, dc), device_id_type=pl.DeviceIdType.MESH,
        )

    def put(here, src, dst, send, recv, dp, dc):
        @pl.when(jnp.logical_not(here))
        def _():
            remote(src, dst, send, recv, dp, dc).start()

        @pl.when(here)
        def _():
            pltpu.make_async_copy(src, dst, recv).start()

    def drain(ref, sem):
        pltpu.make_async_copy(ref, ref, sem).wait()

    def drain_bytes(n, sem):
        drain(bs.at[pl.ds(0, n // 512)], sem)

    barrier = pltpu.get_barrier_semaphore()
    for k in range(1, 16):
        for dev in ((p ^ (k >> 2), by_s(k & 3)), (p, by_xy(k))):
            pl.semaphore_signal(
                barrier, inc=1, device_id=dev, device_id_type=pl.DeviceIdType.MESH
            )
    gap = jnp.full((8, 128), ce_ref[0], F32) - jnp.full((8, 128), ve_ref[0], F32)
    facs[...] = jnp.sqrt((1.0 / gap) * (1.0 / (math.sqrt(256.0) * GRID)))
    for i in range(32):
        wide[i : i + 1, :] = val_in[0:1, 128 * i : 128 * i + 128].astype(F32)
    val_ref[...] = wide[...].astype(BF)
    pl.semaphore_wait(barrier, 30)

    half = lambda h: pl.ds(pl.multiple_of(h * 256, 256), 256)
    mine = vf.at[y, zl, x, core]
    put(twin, val_ref, mine, s_val.at[0], r_val, p, at_s(p))
    for k in range(1, 4):
        remote(val_ref, mine, s_val.at[1], r_val, p ^ k, at_s(p)).start()
    put(twin, facs, fac, s_fac, r_fac, s, at_s(p))
    gone = (s - p) & 3
    near = jnp.where(zl == 0, gone >> 1, 1 - (((gone + 1) >> 1) & 1))
    for h in range(2):
        put(
            twin & (core == h), cond_ref.at[half(h)], cf.at[p, half(h)],
            s_cond.at[h], r_cond.at[p], s, at_s(near * 2 + h),
        )

    drain(vf.at[y, :, x], r_val)
    for k in range(1, 4):
        remote(vf.at[y, 0, x], vf.at[y, 0, x], s_vf, r_va, p, by_xy(k)).start()
        remote(vf.at[y, 1, x], vf.at[y, 1, x], s_vf, r_vb, p, by_xy(4 * k)).start()
    drain_bytes(3 * 16384, r_va)
    for k in range(1, 4):
        remote(vf.at[y, 0], vf.at[y, 0], s_vf, r_vy.at[y], p, by_xy(4 * k)).start()
    drain_bytes(3 * 16384, r_vb)
    for k in range(1, 4):
        remote(vf.at[:, 1, x], vf.at[:, 1, x], s_vf, r_vx, p, by_xy(k)).start()

    e1 = jnp.where(p < 2, 2 * zl, 1 + 2 * zl)

    def pass_on(k):
        q = (p - e1 - k) & 3
        part = cf.at[q, half(core)]
        drain(part, r_cond.at[q])
        if k < 2:
            remote(part, part, s_pass, r_cond.at[q], p, c ^ 8).start()
        remote(part, part, s_sib, r_sib.at[q], p, by_s(1)).start()

    pass_on(0)
    pass_on(1)
    order_planes(plane_ref, ix)
    compose_columns(plane_ref, col_ref, ix)
    fold_indices(ix, fx)
    pass_on(2)
    pass_on(3)

    def ready(n):
        o0 = y ^ (2 * (n & 1))
        o1 = o0 ^ 1
        h = core ^ (n >> 1)
        later = (n & 1) == 1

        @pl.when((h == 0) & later)
        def _():
            drain(vf.at[o0, 0], r_vy.at[o0])

        @pl.when(h == 0)
        def _():
            drain(vf.at[o1, 0], r_vy.at[o1])

        @pl.when((h == 1) & jnp.logical_not(later))
        def _():
            drain_bytes(3 * 65536, r_vx)

        @pl.when(n >= 2)
        def _():
            drain(cf.at[o0, half(1 - core)], r_sib.at[o0])
            drain(cf.at[o1, half(1 - core)], r_sib.at[o1])

        return (o0, h), (o1, h)

    transform(ready, vf, cf, tz, ty, tw, bs)
    drain(fac, r_fac)
    lines_of(fac, tx, bs, wt, sp)

    def keep(t, at, step):
        re, im = pick_tile(t, fx, wt, sp)
        pv[pl.ds(at, 1), :] = re[:, :128]
        pv[pl.ds(at + 1, 1), :] = re[:, 128:]
        pv[pl.ds(at + step, 1), :] = im[:, :128]
        pv[pl.ds(at + step + 1, 1), :] = im[:, 128:]

    for t in range(8):
        keep(t, (t // 2) * 8 + (t % 2) * 2, 4)

    slot = lambda n, size: pl.ds(pl.multiple_of(n * size, size), size)
    mine_cb = cb.at[slot(core * 4 + p, 8)]
    for k in range(8):
        to = base + (zl ^ (k & 1)) * 8 + zl
        src = pv.at[slot(p ^ (k >> 1), 8)]
        if k == 0:
            put(core == zl, src, mine_cb, s_cb.at[0], r_cb, p, to)
        else:
            remote(src, mine_cb, s_cb.at[1], r_cb, p ^ (k >> 1), to).start()

    def columns():
        drain(cb, r_cb)
        own = [(-cb[pl.ds(n, 16, stride=4), :]).astype(BF) for n in range(4)]
        cx[pl.ds(xy, 1), pl.ds(core, 1)] = jnp.concatenate(own, 1)[None, None]
        for k in range(1, 16):
            remote(cx.at[xy, core], cx.at[xy, core], s_cx, r_cx, p, by_xy(k)).start()

    def swap_columns():
        drain_bytes(15 * 16384, r_cx)
        remote(cx.at[:, core], cx.at[:, core], s_cs, r_cs, p, by_s(1)).start()

    def send_rows(h, whole):
        for j in range(16):
            if whole:
                v = rz[j, 0:80].astype(F32)[40 * h : 40 * h + 40]
            else:
                v = rz[j, 48 * h : 48 * h + 48].astype(F32)[:40]
            rf[40 * j : 40 * j + 40, :] = v
        low = lanes((32, 128)) < 64
        for m in range(4):
            a = [rf[pl.ds(5 * m + n, 32, stride=20), :] for n in range(5)]
            b = [pltpu.roll(v, 64, 1) for v in a[2:]]
            odd = [jnp.where(low, b[0], b[1]), jnp.where(low, b[1], b[2]), b[2]]
            xs[8 * h + 2 * m] = jnp.concatenate(a[:3], 1).astype(BF)
            xs[8 * h + 2 * m + 1] = jnp.concatenate(odd, 1).astype(BF)
        for k in range(8):
            o = 8 * h + (k ^ (xy & 7))

            @pl.when(o != xy)
            def _():
                remote(xs.at[o], rx.at[xy], s_rx, r_rx, p, cond_of(o)).start()

            @pl.when(o == xy)
            def _():
                rx[pl.ds(xy, 1)] = xs[pl.ds(xy, 1)]

    def rows_to(g, src, dst, recv):
        put(g == s, src, dst, s_rz, recv, p, at_s(g))
        for j in range(1, 4):
            remote(src, dst, s_rz, recv, p ^ j, at_s(g)).start()

    swap = lambda n: ((n & 1) << 1) | (n >> 1)

    def pick(b, carry):
        k, w = b // 2, b % 2
        g = swap(k)
        for e in range(10):
            keep(8 + g * 20 + w * 10 + e, 32 + w * 40 + 2 * e, 20)

        @pl.when(b == 3)
        def _():
            columns()

        @pl.when((w == 1) & (k < 3))
        def _():
            zs[pl.ds(k, 1), 0:80] = pv[32:112, :].astype(BF)[None]
            rows_to(g, zs.at[k, 0:80], rz.at[me, 0:80], r_rz)

        @pl.when(b == 6)
        def _():
            zs[3, 0:48] = pv[32:80, :].astype(BF)
            rows_to(3, zs.at[3, 0:48], rz.at[me, 0:48], r_rz)

        @pl.when(b == 7)
        def _():
            zs[3, 48:96] = pv[72:120, :].astype(BF)
            rows_to(3, zs.at[3, 48:96], rz.at[me, 48:96], r_rw)

        @pl.when((w == 1) & (k == swap(s) + 2))
        def _():
            drain(rz.at[:, 0:80], r_rz)
            send_rows(0, True)
            send_rows(1, True)

        return carry

    lax.fori_loop(0, 8, pick, 0)

    swap_columns()

    @pl.when(s == 1)
    def _():
        drain(rz.at[:, 0:80], r_rz)
        send_rows(0, True)
        send_rows(1, True)

    @pl.when(s == 3)
    def _():
        drain(rz.at[:, 0:48], r_rz)
        send_rows(0, False)
        drain(rz.at[:, 48:96], r_rw)
        send_rows(1, False)

    drain_bytes(3 * 8192, s_val.at[1])
    for h in range(2):

        @pl.when(jnp.logical_not(twin & (core == h)))
        def _():
            drain(cond_ref.at[half(h)], s_cond.at[h])

    @pl.when(jnp.logical_not(twin))
    def _():
        drain(val_ref, s_val.at[0])
        drain(facs, s_fac)

    drain_bytes(2 * 65536, s_pass)

    drain_bytes(4 * 65536, s_sib)
    drain_bytes(6 * 16384 + 6 * 65536, s_vf)
    drain_bytes(7 * 4096, s_cb.at[1])

    @pl.when(core != zl)
    def _():
        drain_bytes(4096, s_cb.at[0])

    drain_bytes(15 * 16384, s_cx)
    drain(cx.at[:, core], s_cs)

    @pl.when(s < 3)
    def _():
        drain_bytes(316 * 1024, s_rz)

    @pl.when(s == 3)
    def _():
        drain_bytes(312 * 1024, s_rz)

    drain(cx.at[:, 1 - core], r_cs)
    drain_bytes(15 * 24576, r_rx)
    drain_bytes(15 * 24576, s_rx)


def on_device(val_orbitals, cond_orbitals, val_energy, cond_energy, plane_index, column_index):
    vmem = pl.BlockSpec(memory_space=pltpu.VMEM)
    smem = pl.BlockSpec(memory_space=pltpu.SMEM)
    dma = lambda *n: pltpu.SemaphoreType.DMA(n) if n else pltpu.SemaphoreType.DMA
    rx, cx = pl.pallas_call(
        kernel,
        out_shape=(
            jax.ShapeDtypeStruct((16, 32, 384), BF),
            jax.ShapeDtypeStruct((16, 2, 16, 512), BF),
        ),
        in_specs=[vmem, vmem, smem, smem] + [vmem] * 6,
        out_specs=(vmem, vmem),
        scratch_shapes=[
            pltpu.VMEM((32, 128), BF),
            pltpu.VMEM((32, 128), F32),
            pltpu.VMEM((4, 2, 4, 2, 32, 128), BF),
            pltpu.VMEM((4, 512, 128), BF),
            pltpu.VMEM((8, 128), F32),
            pltpu.VMEM((8, 128), F32),
            pltpu.VMEM((176, 128), jnp.int32),
            pltpu.VMEM((6, 176, 128), F32),
            pltpu.VMEM((4096, 128), F32),
            pltpu.VMEM((512, 512), BF),
            pltpu.VMEM((8, 256), F32),
            pltpu.VMEM((128, 128), F32),
            pltpu.VMEM((64, 128), F32),
            pltpu.VMEM((4, 96, 128), BF),
            pltpu.VMEM((16, 96, 128), BF),
            pltpu.VMEM((1280, 128), F32),
            pltpu.VMEM((16, 32, 384), BF),
            dma(2), dma(), dma(2), dma(4), dma(), dma(), dma(4), dma(), dma(),
            dma(), dma(), dma(), dma(4), dma(),
            dma(2), dma(), dma(), dma(), dma(), dma(), dma(), dma(), dma(), dma(), dma(),
        ],
        compiler_params=pltpu.CompilerParams(
            collective_id=0, has_side_effects=True, vmem_limit_bytes=48 * 2**20
        ),
        name="polarizability",
    )(
        val_orbitals,
        cond_orbitals.reshape(512, 128),
        val_energy,
        cond_energy,
        plane_index.reshape(156, 128),
        column_index.reshape(16, 128),
        *[jnp.asarray(t) for t in tables()],
    )
    return lax.dot_general(
        rx.reshape(512, 384)[:, :ROWS], cx.reshape(512, 512), (((0,), (0,)), ((), ())),
        preferred_element_type=F32,
    )


def solution(mesh):
    placed = (P("val", "cond"), P("cond", "val"), P("val"), P("cond"), P(), P())
    return jax.shard_map(
        on_device, mesh=mesh, in_specs=placed, out_specs=P("cond", "val"), check_vma=False
    )
```

```python
import math

import jax
import jax.numpy as jnp
import ml_dtypes
import numpy as np
from jax import lax
from jax.experimental import pallas as pl
from jax.experimental.pallas import tpu as pltpu
from jax.sharding import PartitionSpec as P

N = 64
GRID = N**3
BF = jnp.bfloat16
F32 = jnp.float32
ROWS = 312


def split(a):
    hi = a.astype(ml_dtypes.bfloat16)
    return hi, (a - hi.astype(np.float64)).astype(ml_dtypes.bfloat16)


def tables():
    k = np.arange(N)
    ang = 2 * np.pi * (k[:, None] * k[None, :] % N) / N
    cos, sin = np.cos(ang), np.sin(ang)
    tz = np.zeros((2, N, 2, 2, N))
    for par in range(2):
        tz[par, :, 0, par, :] = cos
        tz[par, :, 1, par, :] = -sin
    tz = tz.reshape(128, 256)
    tz = np.concatenate([tz, tz], 0).astype(ml_dtypes.bfloat16)
    h = np.arange(32)
    ang = 2 * np.pi * (h[:, None] * h[None, :] % 32) / 32
    ty = np.block([[np.cos(ang), np.sin(ang)], [-np.sin(ang), np.cos(ang)]])
    hi, lo = split(ty)
    ty = np.concatenate([hi, lo, hi], 1)
    tx = np.zeros((80, 128))
    tx[:32, :64], tx[:32, 64:] = cos[:32], sin[:32]
    tx[32:64, :64], tx[32:64, 64:] = -sin[:32], cos[:32]
    tx[64, :64] = cos[32]
    tx[65, 64:] = cos[32]
    tx = np.concatenate([tx, tx], 1).astype(ml_dtypes.bfloat16)
    tw = np.zeros((2, 32, 128), np.float32)
    tw[0, :, :64] = 1.0
    ang = 2 * np.pi * h / N
    tw[0, :, 64:] = np.cos(ang)[:, None]
    tw[1, :, 64:] = -np.sin(ang)[:, None]
    return tz, ty, tx, tw


def cond_id(s, xy):
    return (xy // 4) * 16 + (s // 2) * 8 + (xy % 4) * 2 + s % 2


def lanes(shape):
    return lax.broadcasted_iota(jnp.int32, shape, len(shape) - 1)


def subl(shape):
    return lax.broadcasted_iota(jnp.int32, shape, len(shape) - 2)


def order_planes(plane_ref, ix_ref):
    lane = lanes((3, 128))

    def take(start):
        row, off = start // 128, start % 128
        a = plane_ref[row : row + 3, :]
        if off:
            if row + 4 <= 156:
                b = plane_ref[row + 1 : row + 4, :]
            else:
                b = jnp.concatenate([plane_ref[row + 1 : row + 3, :], a[2:3]], 0)
            a = jnp.where(lane < 128 - off, pltpu.roll(a, 128 - off, 1), pltpu.roll(b, 128 - off, 1))
        return a

    for s in range(4):
        for m in range(8):
            even = take(ROWS * cond_id(s, 2 * m))
            odd = take(ROWS * cond_id(s, 2 * m + 1) - 64)
            at = 16 + s * 40 + m * 5
            ix_ref[at : at + 2, :] = even[:2]
            ix_ref[at + 2 : at + 3, :] = jnp.where(lane[:1] < 64, even[2:], odd[:1])
            ix_ref[at + 3 : at + 5, :] = odd[1:]


def compose_columns(plane_ref, col_ref, ix_ref):
    plane = jnp.concatenate([plane_ref[...], jnp.zeros((100, 128), jnp.int32)], 0)
    digits = [
        jnp.transpose(((plane >> sh) & 63).astype(F32), (1, 0)).astype(BF) for sh in (12, 6, 0)
    ]
    left = jnp.concatenate(digits, 0)

    def tile(t, carry):
        col = jnp.concatenate([col_ref[pl.ds(2 * t, 1), :], col_ref[pl.ds(2 * t + 1, 1), :]], 1)
        hot = jnp.where(subl((256, 256)) == (col >> 7), 1.0, 0.0).astype(BF)
        prod = jnp.dot(left, hot, preferred_element_type=F32)
        mask = subl((128, 256)) == (col & 127)
        kx, ky, kz = [
            jnp.sum(jnp.where(mask, prod[128 * d : 128 * d + 128], 0.0), axis=0, keepdims=True)
            for d in range(3)
        ]
        flat = (kx * 4096.0 + ky * 64.0 + kz).astype(jnp.int32)
        ix_ref[pl.ds(2 * t, 1), :] = flat[:, :128]
        ix_ref[pl.ds(2 * t + 1, 1), :] = flat[:, 128:]
        return carry

    lax.fori_loop(0, 8, tile, 0, unroll=8)


def fold_indices(ix_ref, fx_ref):
    n = ix_ref[...]
    kx, ky, kz = n >> 12, (n >> 6) & 63, n & 63
    low = (kx & 31) == 0
    yline = (ky & 31) == 0
    zpoint = (kz & 31) == 0
    neg = kx > 32
    neg = neg | (low & ~yline & ((kx == 0) == (ky > 32)))
    neg = neg | (low & yline & ~zpoint & ((ky == 0) == (kz > 32)))
    special = low & yline & zpoint & ((ky == 0) == (kz == 32))
    turn = lambda k: jnp.where(neg, (64 - k) & 63, k)
    kx, ky, kz = turn(kx), turn(ky), turn(kz)
    slot_y = jnp.where(low & yline, kx, ky)
    fx_ref[0] = (kx & 31).astype(F32)
    fx_ref[1] = jnp.where(special, 99, slot_y & 15).astype(F32)
    line = ((slot_y >> 4) & 1) * 128 + (slot_y >> 5) * 64 + kz
    fx_ref[2] = (line & 15).astype(F32)
    fx_ref[5] = (line >> 4).astype(F32)
    fx_ref[3] = jnp.where(neg, -1.0, 1.0)
    fx_ref[4] = jnp.where(special, (kx >> 5) * 2 + (ky >> 5), 9).astype(F32)


def transform(ready, vf, cf, tz, ty, tw, bs):
    low = lanes((32, 128)) < 64

    def planes(n, carry):
        for y, zl in ready(n):
            a = vf[y, zl].reshape(256, 128).astype(F32)
            b = cf[y, pl.ds(pl.multiple_of(zl * 256, 256), 256), :].astype(F32)
            d = a * b
            hi = d.astype(BF)
            lo = (d - hi.astype(F32)).astype(BF)
            az = jnp.dot(jnp.concatenate([hi, lo], 1), tz[...], preferred_element_type=F32)
            for m in range(4):
                cols = []
                for x in (2 * m, 2 * m + 1):
                    blk = az[x * 32 : x * 32 + 32]
                    cols.append(jnp.concatenate([blk[:, :128], blk[:, 128:]], 0))
                r = jnp.concatenate(cols, 1)
                hi = r.astype(BF)
                lo = (r - hi.astype(F32)).astype(BF)
                g = jnp.dot(ty[...], jnp.concatenate([hi, hi, lo], 0), preferred_element_type=F32)
                for e in range(2):
                    gr, gi = g[:32, e * 128 : e * 128 + 128], g[32:, e * 128 : e * 128 + 128]
                    yr = gr * tw[0] - gi * tw[1]
                    yi = gr * tw[1] + gi * tw[0]
                    at = (y * 16 + zl * 8 + 2 * m + e) * 32
                    for part, v in ((0, yr), (1, yi)):
                        rv = pltpu.roll(v, 64, 1)
                        out = jnp.where(low, rv + v, rv - v)
                        bs[pl.ds(pl.multiple_of(part * 2048 + at, 32), 32), :] = out
        return carry

    lax.fori_loop(0, 4, planes, 0)


def lines_of(fac_ref, tx, bs, wt, sp):
    fac = fac_ref[0:1, :]

    def lines(i, carry):
        b = [bs[pl.ds(4 * i + j, 128, stride=32), :] for j in range(4)]
        r = jnp.concatenate(b, 1)
        hi = r.astype(BF)
        lo = (r - hi.astype(F32)).astype(BF)
        f = jnp.dot(tx[...], jnp.concatenate([hi, lo], 0), preferred_element_type=F32)
        lane = lanes((1, 128))
        top = subl((32, 128)) == 0
        for part in range(2):
            blocks = []
            for j in range(4):
                main = f[32 * part : 32 * part + 32, 128 * j : 128 * j + 128] * fac
                edge = f[64 + part : 65 + part, 128 * j : 128 * j + 128] * fac
                row = main[0:1]
                new = jnp.where(lane < 64, row, edge)
                if j == 0:
                    first = jnp.where(
                        lane < 32,
                        row,
                        jnp.where(
                            lane < 64,
                            pltpu.roll(row, 64, 1),
                            jnp.where(lane < 96, pltpu.roll(edge, 64, 1), edge),
                        ),
                    )
                    if part == 0:

                        @pl.when(i == 0)
                        def _():
                            for n, (v, at) in enumerate(
                                ((row, 32), (row, 64), (edge, 32), (edge, 64))
                            ):
                                pick = jnp.sum(
                                    jnp.where(lane == at, v, 0.0), axis=1, keepdims=True
                                )
                                pick = pick.astype(BF).astype(F32)
                                sp[n : n + 1, :] = jnp.broadcast_to(pick, (1, 256))

                    new = jnp.where(i == 0, first, new)
                blocks.append(jnp.where(top, jnp.broadcast_to(new, (32, 128)), main))
            whole = jnp.transpose(jnp.concatenate(blocks, 0), (1, 0)).astype(BF)
            rows = pl.ds(pl.multiple_of(256 * part + (i // 4) * 128, 128), 128)
            wt[rows, pl.ds(pl.multiple_of((i % 4) * 128, 128), 128)] = whole
        return carry

    lax.fori_loop(0, 8, lines, 0, unroll=4)


def pick_tile(t, fx, wt, sp):
    def row(n):
        return jnp.concatenate([fx[n, pl.ds(2 * t, 1), :], fx[n, pl.ds(2 * t + 1, 1), :]], 1)

    kx = jnp.broadcast_to(row(0), (32, 256)).astype(BF)
    ky = jnp.broadcast_to(row(1), (16, 256)).astype(BF)
    index = subl((32, 256)).astype(F32).astype(BF)
    one, zero = jnp.ones((32, 256), BF), jnp.zeros((16, 256), BF)
    base = jnp.where(kx == index, one, jnp.zeros((32, 256), BF))
    hot = []
    for j in range(16):
        here = ky == jnp.asarray(j, BF)
        hot += [jnp.where(here, base[:16], zero), jnp.where(here, base[16:], zero)]
    hot = jnp.concatenate(hot, 0)
    prod = jnp.dot(wt[...], hot, preferred_element_type=F32).astype(BF)
    high = jnp.broadcast_to(row(5), (16, 256)).astype(BF)
    chosen = [prod[:16], prod[256:272]]
    for n in range(1, 16):
        here = high == jnp.asarray(n, BF)
        for part in range(2):
            at = 256 * part + 16 * n
            chosen[part] = jnp.where(here, prod[at : at + 16], chosen[part])
    line = subl((16, 256)).astype(F32) == row(2)
    re, im = [
        jnp.sum(jnp.where(line, v.astype(F32), 0.0), axis=0, keepdims=True) for v in chosen
    ]
    kind = row(4)
    for n in range(4):
        re = jnp.where(kind == float(n), sp[n : n + 1, :], re)
    return re, im * row(3)


def kernel(
    val_in, cond_ref, ve_ref, ce_ref, plane_ref, col_ref, tz, ty, tx, tw,
    rx, cx,
    val_ref, wide, vf, cf, facs, fac, ix, fx, bs, wt, sp, pv, cb, zs, rz, rf, xs,
    s_val, r_val, s_cond, r_cond, s_pass, s_sib, r_sib, s_fac, r_fac,
    s_vf, r_va, r_vb, r_vy, r_vx,
    s_cb, r_cb, s_cx, r_cx, s_cs, r_cs, s_rz, r_rz, r_rw, s_rx, r_rx,
):
    p = lax.axis_index("val")
    c = lax.axis_index("cond")
    y, zl, x, core = c // 16, (c // 8) % 2, (c // 2) % 4, c % 2
    s = zl * 2 + core
    xy = y * 4 + x
    me = s * 4 + p
    base = y * 16 + x * 2
    at_s = lambda n: base + (n >> 1) * 8 + (n & 1)
    by_s = lambda k: c ^ (((k >> 1) << 3) | (k & 1))
    by_xy = lambda k: c ^ (((k >> 2) << 4) | ((k & 3) << 1))
    twin = p == s
    cond_of = lambda o: (c & 9) | ((o >> 2) << 4) | ((o & 3) << 1)

    def remote(src, dst, send, recv, dp, dc):
        return pltpu.make_async_remote_copy(
            src_ref=src, dst_ref=dst, send_sem=send, recv_sem=recv,
            device_id=(dp, dc), device_id_type=pl.DeviceIdType.MESH,
        )

    def put(here, src, dst, send, recv, dp, dc):
        @pl.when(jnp.logical_not(here))
        def _():
            remote(src, dst, send, recv, dp, dc).start()

        @pl.when(here)
        def _():
            pltpu.make_async_copy(src, dst, recv).start()

    def drain(ref, sem):
        pltpu.make_async_copy(ref, ref, sem).wait()

    def drain_bytes(n, sem):
        drain(bs.at[pl.ds(0, n // 512)], sem)

    barrier = pltpu.get_barrier_semaphore()
    for k in range(1, 16):
        for dev in ((p ^ (k >> 2), by_s(k & 3)), (p, by_xy(k))):
            pl.semaphore_signal(
                barrier, inc=1, device_id=dev, device_id_type=pl.DeviceIdType.MESH
            )
    gap = jnp.full((8, 128), ce_ref[0], F32) - jnp.full((8, 128), ve_ref[0], F32)
    facs[...] = jnp.sqrt((1.0 / gap) * (1.0 / (math.sqrt(256.0) * GRID)))
    for i in range(32):
        wide[i : i + 1, :] = val_in[0:1, 128 * i : 128 * i + 128].astype(F32)
    val_ref[...] = wide[...].astype(BF)
    pl.semaphore_wait(barrier, 30)

    half = lambda h: pl.ds(pl.multiple_of(h * 256, 256), 256)
    mine = vf.at[y, zl, x, core]
    put(twin, val_ref, mine, s_val.at[0], r_val, p, at_s(p))
    for k in range(1, 4):
        remote(val_ref, mine, s_val.at[1], r_val, p ^ k, at_s(p)).start()
    put(twin, facs, fac, s_fac, r_fac, s, at_s(p))
    gone = (s - p) & 3
    near = jnp.where(zl == 0, gone >> 1, 1 - (((gone + 1) >> 1) & 1))
    for h in range(2):
        put(
            twin & (core == h), cond_ref.at[half(h)], cf.at[p, half(h)],
            s_cond.at[h], r_cond.at[p], s, at_s(near * 2 + h),
        )

    drain(vf.at[y, :, x], r_val)
    for k in range(1, 4):
        remote(vf.at[y, 0, x], vf.at[y, 0, x], s_vf, r_va, p, by_xy(k)).start()
        remote(vf.at[y, 1, x], vf.at[y, 1, x], s_vf, r_vb, p, by_xy(4 * k)).start()
    drain_bytes(3 * 16384, r_va)
    for k in range(1, 4):
        remote(vf.at[y, 0], vf.at[y, 0], s_vf, r_vy.at[y], p, by_xy(4 * k)).start()
    drain_bytes(3 * 16384, r_vb)
    for k in range(1, 4):
        remote(vf.at[:, 1, x], vf.at[:, 1, x], s_vf, r_vx, p, by_xy(k)).start()

    e1 = jnp.where(p < 2, 2 * zl, 1 + 2 * zl)

    def pass_on(k):
        q = (p - e1 - k) & 3
        part = cf.at[q, half(core)]
        drain(part, r_cond.at[q])
        if k < 2:
            remote(part, part, s_pass, r_cond.at[q], p, c ^ 8).start()
        remote(part, part, s_sib, r_sib.at[q], p, by_s(1)).start()

    pass_on(0)
    pass_on(1)
    order_planes(plane_ref, ix)
    compose_columns(plane_ref, col_ref, ix)
    fold_indices(ix, fx)
    pass_on(2)
    pass_on(3)

    def ready(n):
        o0 = y ^ (2 * (n & 1))
        o1 = o0 ^ 1
        h = core ^ (n >> 1)
        later = (n & 1) == 1

        @pl.when((h == 0) & later)
        def _():
            drain(vf.at[o0, 0], r_vy.at[o0])

        @pl.when(h == 0)
        def _():
            drain(vf.at[o1, 0], r_vy.at[o1])

        @pl.when((h == 1) & jnp.logical_not(later))
        def _():
            drain_bytes(3 * 65536, r_vx)

        @pl.when(n >= 2)
        def _():
            drain(cf.at[o0, half(1 - core)], r_sib.at[o0])
            drain(cf.at[o1, half(1 - core)], r_sib.at[o1])

        return (o0, h), (o1, h)

    transform(ready, vf, cf, tz, ty, tw, bs)
    drain(fac, r_fac)
    lines_of(fac, tx, bs, wt, sp)

    def keep(t, at, step):
        re, im = pick_tile(t, fx, wt, sp)
        pv[pl.ds(at, 1), :] = re[:, :128]
        pv[pl.ds(at + 1, 1), :] = re[:, 128:]
        pv[pl.ds(at + step, 1), :] = im[:, :128]
        pv[pl.ds(at + step + 1, 1), :] = im[:, 128:]

    for t in range(8):
        keep(t, (t // 2) * 8 + (t % 2) * 2, 4)

    slot = lambda n, size: pl.ds(pl.multiple_of(n * size, size), size)
    mine_cb = cb.at[slot(core * 4 + p, 8)]
    for k in range(8):
        to = base + (zl ^ (k & 1)) * 8 + zl
        src = pv.at[slot(p ^ (k >> 1), 8)]
        if k == 0:
            put(core == zl, src, mine_cb, s_cb.at[0], r_cb, p, to)
        else:
            remote(src, mine_cb, s_cb.at[1], r_cb, p ^ (k >> 1), to).start()

    def columns():
        drain(cb, r_cb)
        own = [(-cb[pl.ds(n, 16, stride=4), :]).astype(BF) for n in range(4)]
        cx[pl.ds(xy, 1), pl.ds(core, 1)] = jnp.concatenate(own, 1)[None, None]
        for k in range(1, 16):
            remote(cx.at[xy, core], cx.at[xy, core], s_cx, r_cx, p, by_xy(k)).start()

    def swap_columns():
        drain_bytes(15 * 16384, r_cx)
        remote(cx.at[:, core], cx.at[:, core], s_cs, r_cs, p, by_s(1)).start()

    def send_rows(h, whole):
        for j in range(16):
            if whole:
                v = rz[j, 0:80].astype(F32)[40 * h : 40 * h + 40]
            else:
                v = rz[j, 48 * h : 48 * h + 48].astype(F32)[:40]
            rf[40 * j : 40 * j + 40, :] = v
        low = lanes((32, 128)) < 64
        for m in range(4):
            a = [rf[pl.ds(5 * m + n, 32, stride=20), :] for n in range(5)]
            b = [pltpu.roll(v, 64, 1) for v in a[2:]]
            odd = [jnp.where(low, b[0], b[1]), jnp.where(low, b[1], b[2]), b[2]]
            xs[8 * h + 2 * m] = jnp.concatenate(a[:3], 1).astype(BF)
            xs[8 * h + 2 * m + 1] = jnp.concatenate(odd, 1).astype(BF)
        for k in range(8):
            o = 8 * h + (k ^ (xy & 7))

            @pl.when(o != xy)
            def _():
                remote(xs.at[o], rx.at[xy], s_rx, r_rx, p, cond_of(o)).start()

            @pl.when(o == xy)
            def _():
                rx[pl.ds(xy, 1)] = xs[pl.ds(xy, 1)]

    def rows_to(g, src, dst, recv):
        put(g == s, src, dst, s_rz, recv, p, at_s(g))
        for j in range(1, 4):
            remote(src, dst, s_rz, recv, p ^ j, at_s(g)).start()

    swap = lambda n: ((n & 1) << 1) | (n >> 1)

    def pick(b, carry):
        k, w = b // 2, b % 2
        g = swap(k)
        for e in range(10):
            keep(8 + g * 20 + w * 10 + e, 32 + w * 40 + 2 * e, 20)

        @pl.when(b == 3)
        def _():
            columns()

        @pl.when((w == 1) & (k < 3))
        def _():
            zs[pl.ds(k, 1), 0:80] = pv[32:112, :].astype(BF)[None]
            rows_to(g, zs.at[k, 0:80], rz.at[me, 0:80], r_rz)

        @pl.when(b == 6)
        def _():
            zs[3, 0:48] = pv[32:80, :].astype(BF)
            rows_to(3, zs.at[3, 0:48], rz.at[me, 0:48], r_rz)

        @pl.when(b == 7)
        def _():
            zs[3, 48:96] = pv[72:120, :].astype(BF)
            rows_to(3, zs.at[3, 48:96], rz.at[me, 48:96], r_rw)

        @pl.when((w == 1) & (k == swap(s) + 2))
        def _():
            drain(rz.at[:, 0:80], r_rz)
            send_rows(0, True)
            send_rows(1, True)

        return carry

    lax.fori_loop(0, 8, pick, 0)

    swap_columns()

    @pl.when(s == 1)
    def _():
        drain(rz.at[:, 0:80], r_rz)
        send_rows(0, True)
        send_rows(1, True)

    @pl.when(s == 3)
    def _():
        drain(rz.at[:, 0:48], r_rz)
        send_rows(0, False)
        drain(rz.at[:, 48:96], r_rw)
        send_rows(1, False)

    drain_bytes(3 * 8192, s_val.at[1])
    for h in range(2):

        @pl.when(jnp.logical_not(twin & (core == h)))
        def _():
            drain(cond_ref.at[half(h)], s_cond.at[h])

    @pl.when(jnp.logical_not(twin))
    def _():
        drain(val_ref, s_val.at[0])
        drain(facs, s_fac)

    drain_bytes(2 * 65536, s_pass)

    drain_bytes(4 * 65536, s_sib)
    drain_bytes(6 * 16384 + 6 * 65536, s_vf)
    drain_bytes(7 * 4096, s_cb.at[1])

    @pl.when(core != zl)
    def _():
        drain_bytes(4096, s_cb.at[0])

    drain_bytes(15 * 16384, s_cx)
    drain(cx.at[:, core], s_cs)

    @pl.when(s < 3)
    def _():
        drain_bytes(316 * 1024, s_rz)

    @pl.when(s == 3)
    def _():
        drain_bytes(312 * 1024, s_rz)

    drain(cx.at[:, 1 - core], r_cs)
    drain_bytes(15 * 24576, r_rx)
    drain_bytes(15 * 24576, s_rx)


def on_device(val_orbitals, cond_orbitals, val_energy, cond_energy, plane_index, column_index):
    vmem = pl.BlockSpec(memory_space=pltpu.VMEM)
    smem = pl.BlockSpec(memory_space=pltpu.SMEM)
    dma = lambda *n: pltpu.SemaphoreType.DMA(n) if n else pltpu.SemaphoreType.DMA
    rx, cx = pl.pallas_call(
        kernel,
        out_shape=(
            jax.ShapeDtypeStruct((16, 32, 384), BF),
            jax.ShapeDtypeStruct((16, 2, 16, 512), BF),
        ),
        in_specs=[vmem, vmem, smem, smem] + [vmem] * 6,
        out_specs=(vmem, vmem),
        scratch_shapes=[
            pltpu.VMEM((32, 128), BF),
            pltpu.VMEM((32, 128), F32),
            pltpu.VMEM((4, 2, 4, 2, 32, 128), BF),
            pltpu.VMEM((4, 512, 128), BF),
            pltpu.VMEM((8, 128), F32),
            pltpu.VMEM((8, 128), F32),
            pltpu.VMEM((176, 128), jnp.int32),
            pltpu.VMEM((6, 176, 128), F32),
            pltpu.VMEM((4096, 128), F32),
            pltpu.VMEM((512, 512), BF),
            pltpu.VMEM((8, 256), F32),
            pltpu.VMEM((128, 128), F32),
            pltpu.VMEM((64, 128), F32),
            pltpu.VMEM((4, 96, 128), BF),
            pltpu.VMEM((16, 96, 128), BF),
            pltpu.VMEM((1280, 128), F32),
            pltpu.VMEM((16, 32, 384), BF),
            dma(2), dma(), dma(2), dma(4), dma(), dma(), dma(4), dma(), dma(),
            dma(), dma(), dma(), dma(4), dma(),
            dma(2), dma(), dma(), dma(), dma(), dma(), dma(), dma(), dma(), dma(), dma(),
        ],
        compiler_params=pltpu.CompilerParams(
            collective_id=0, has_side_effects=True, vmem_limit_bytes=48 * 2**20
        ),
        name="polarizability",
    )(
        val_orbitals,
        cond_orbitals.reshape(512, 128),
        val_energy,
        cond_energy,
        plane_index.reshape(156, 128),
        column_index.reshape(16, 128),
        *[jnp.asarray(t) for t in tables()],
    )
    return lax.dot_general(
        rx.reshape(512, 384)[:, :ROWS], cx.reshape(512, 512), (((0,), (0,)), ((), ())),
        preferred_element_type=F32,
    )


def solution(mesh):
    placed = (P("val", "cond"), P("cond", "val"), P("val"), P("cond"), P(), P())
    return jax.shard_map(
        on_device, mesh=mesh, in_specs=placed, out_specs=P("cond", "val"), check_vma=False
    )
```

```python
import math

import jax
import jax.numpy as jnp
import ml_dtypes
import numpy as np
from jax import lax
from jax.experimental import pallas as pl
from jax.experimental.pallas import tpu as pltpu
from jax.sharding import PartitionSpec as P

N = 64
GRID = N**3
BF = jnp.bfloat16
F32 = jnp.float32
ROWS = 312


def split(a):
    hi = a.astype(ml_dtypes.bfloat16)
    return hi, (a - hi.astype(np.float64)).astype(ml_dtypes.bfloat16)


def tables():
    k = np.arange(N)
    ang = 2 * np.pi * (k[:, None] * k[None, :] % N) / N
    cos, sin = np.cos(ang), np.sin(ang)
    tz = np.zeros((2, N, 2, 2, N))
    for par in range(2):
        tz[par, :, 0, par, :] = cos
        tz[par, :, 1, par, :] = -sin
    tz = tz.reshape(128, 256)
    tz = np.concatenate([tz, tz], 0).astype(ml_dtypes.bfloat16)
    h = np.arange(32)
    ang = 2 * np.pi * (h[:, None] * h[None, :] % 32) / 32
    ty = np.block([[np.cos(ang), np.sin(ang)], [-np.sin(ang), np.cos(ang)]])
    hi, lo = split(ty)
    ty = np.concatenate([hi, lo, hi], 1)
    tx = np.zeros((80, 128))
    tx[:32, :64], tx[:32, 64:] = cos[:32], sin[:32]
    tx[32:64, :64], tx[32:64, 64:] = -sin[:32], cos[:32]
    tx[64, :64] = cos[32]
    tx[65, 64:] = cos[32]
    tx = np.concatenate([tx, tx], 1).astype(ml_dtypes.bfloat16)
    tw = np.zeros((2, 32, 128), np.float32)
    tw[0, :, :64] = 1.0
    ang = 2 * np.pi * h / N
    tw[0, :, 64:] = np.cos(ang)[:, None]
    tw[1, :, 64:] = -np.sin(ang)[:, None]
    return tz, ty, tx, tw


def cond_id(s, xy):
    return (xy // 4) * 16 + (s // 2) * 8 + (xy % 4) * 2 + s % 2


def lanes(shape):
    return lax.broadcasted_iota(jnp.int32, shape, len(shape) - 1)


def subl(shape):
    return lax.broadcasted_iota(jnp.int32, shape, len(shape) - 2)


def order_planes(plane_ref, ix_ref):
    lane = lanes((3, 128))

    def take(start):
        row, off = start // 128, start % 128
        a = plane_ref[row : row + 3, :]
        if off:
            if row + 4 <= 156:
                b = plane_ref[row + 1 : row + 4, :]
            else:
                b = jnp.concatenate([plane_ref[row + 1 : row + 3, :], a[2:3]], 0)
            a = jnp.where(lane < 128 - off, pltpu.roll(a, 128 - off, 1), pltpu.roll(b, 128 - off, 1))
        return a

    for s in range(4):
        for m in range(8):
            even = take(ROWS * cond_id(s, 2 * m))
            odd = take(ROWS * cond_id(s, 2 * m + 1) - 64)
            at = 16 + s * 40 + m * 5
            ix_ref[at : at + 2, :] = even[:2]
            ix_ref[at + 2 : at + 3, :] = jnp.where(lane[:1] < 64, even[2:], odd[:1])
            ix_ref[at + 3 : at + 5, :] = odd[1:]


def compose_columns(plane_ref, col_ref, ix_ref):
    plane = jnp.concatenate([plane_ref[...], jnp.zeros((100, 128), jnp.int32)], 0)
    digits = [
        jnp.transpose(((plane >> sh) & 63).astype(F32), (1, 0)).astype(BF) for sh in (12, 6, 0)
    ]
    left = jnp.concatenate(digits, 0)

    def tile(t, carry):
        col = jnp.concatenate([col_ref[pl.ds(2 * t, 1), :], col_ref[pl.ds(2 * t + 1, 1), :]], 1)
        hot = jnp.where(subl((256, 256)) == (col >> 7), 1.0, 0.0).astype(BF)
        prod = jnp.dot(left, hot, preferred_element_type=F32)
        mask = subl((128, 256)) == (col & 127)
        kx, ky, kz = [
            jnp.sum(jnp.where(mask, prod[128 * d : 128 * d + 128], 0.0), axis=0, keepdims=True)
            for d in range(3)
        ]
        flat = (kx * 4096.0 + ky * 64.0 + kz).astype(jnp.int32)
        ix_ref[pl.ds(2 * t, 1), :] = flat[:, :128]
        ix_ref[pl.ds(2 * t + 1, 1), :] = flat[:, 128:]
        return carry

    lax.fori_loop(0, 8, tile, 0, unroll=8)


def fold_indices(ix_ref, fx_ref):
    n = ix_ref[...]
    kx, ky, kz = n >> 12, (n >> 6) & 63, n & 63
    low = (kx & 31) == 0
    yline = (ky & 31) == 0
    zpoint = (kz & 31) == 0
    neg = kx > 32
    neg = neg | (low & ~yline & ((kx == 0) == (ky > 32)))
    neg = neg | (low & yline & ~zpoint & ((ky == 0) == (kz > 32)))
    special = low & yline & zpoint & ((ky == 0) == (kz == 32))
    turn = lambda k: jnp.where(neg, (64 - k) & 63, k)
    kx, ky, kz = turn(kx), turn(ky), turn(kz)
    slot_y = jnp.where(low & yline, kx, ky)
    fx_ref[0] = (kx & 31).astype(F32)
    fx_ref[1] = jnp.where(special, 99, slot_y & 15).astype(F32)
    line = ((slot_y >> 4) & 1) * 128 + (slot_y >> 5) * 64 + kz
    fx_ref[2] = (line & 15).astype(F32)
    fx_ref[5] = (line >> 4).astype(F32)
    fx_ref[3] = jnp.where(neg, -1.0, 1.0)
    fx_ref[4] = jnp.where(special, (kx >> 5) * 2 + (ky >> 5), 9).astype(F32)


def transform(ready, vf, cf, tz, ty, tw, bs):
    low = lanes((32, 128)) < 64

    def planes(n, carry):
        for y, zl in ready(n):
            a = vf[y, zl].reshape(256, 128).astype(F32)
            b = cf[y, pl.ds(pl.multiple_of(zl * 256, 256), 256), :].astype(F32)
            d = a * b
            hi = d.astype(BF)
            lo = (d - hi.astype(F32)).astype(BF)
            az = jnp.dot(jnp.concatenate([hi, lo], 1), tz[...], preferred_element_type=F32)
            for m in range(4):
                cols = []
                for x in (2 * m, 2 * m + 1):
                    blk = az[x * 32 : x * 32 + 32]
                    cols.append(jnp.concatenate([blk[:, :128], blk[:, 128:]], 0))
                r = jnp.concatenate(cols, 1)
                hi = r.astype(BF)
                lo = (r - hi.astype(F32)).astype(BF)
                g = jnp.dot(ty[...], jnp.concatenate([hi, hi, lo], 0), preferred_element_type=F32)
                for e in range(2):
                    gr, gi = g[:32, e * 128 : e * 128 + 128], g[32:, e * 128 : e * 128 + 128]
                    yr = gr * tw[0] - gi * tw[1]
                    yi = gr * tw[1] + gi * tw[0]
                    at = (y * 16 + zl * 8 + 2 * m + e) * 32
                    for part, v in ((0, yr), (1, yi)):
                        rv = pltpu.roll(v, 64, 1)
                        out = jnp.where(low, rv + v, rv - v)
                        bs[pl.ds(pl.multiple_of(part * 2048 + at, 32), 32), :] = out
        return carry

    lax.fori_loop(0, 4, planes, 0)


def lines_of(fac_ref, tx, bs, wt, sp):
    fac = fac_ref[0:1, :]

    def lines(i, carry):
        b = [bs[pl.ds(4 * i + j, 128, stride=32), :] for j in range(4)]
        r = jnp.concatenate(b, 1)
        hi = r.astype(BF)
        lo = (r - hi.astype(F32)).astype(BF)
        f = jnp.dot(tx[...], jnp.concatenate([hi, lo], 0), preferred_element_type=F32)
        lane = lanes((1, 128))
        top = subl((32, 128)) == 0
        for part in range(2):
            blocks = []
            for j in range(4):
                main = f[32 * part : 32 * part + 32, 128 * j : 128 * j + 128] * fac
                edge = f[64 + part : 65 + part, 128 * j : 128 * j + 128] * fac
                row = main[0:1]
                new = jnp.where(lane < 64, row, edge)
                if j == 0:
                    first = jnp.where(
                        lane < 32,
                        row,
                        jnp.where(
                            lane < 64,
                            pltpu.roll(row, 64, 1),
                            jnp.where(lane < 96, pltpu.roll(edge, 64, 1), edge),
                        ),
                    )
                    if part == 0:

                        @pl.when(i == 0)
                        def _():
                            for n, (v, at) in enumerate(
                                ((row, 32), (row, 64), (edge, 32), (edge, 64))
                            ):
                                pick = jnp.sum(
                                    jnp.where(lane == at, v, 0.0), axis=1, keepdims=True
                                )
                                pick = pick.astype(BF).astype(F32)
                                sp[n : n + 1, :] = jnp.broadcast_to(pick, (1, 256))

                    new = jnp.where(i == 0, first, new)
                blocks.append(jnp.where(top, jnp.broadcast_to(new, (32, 128)), main))
            whole = jnp.transpose(jnp.concatenate(blocks, 0), (1, 0)).astype(BF)
            rows = pl.ds(pl.multiple_of(256 * part + (i // 4) * 128, 128), 128)
            wt[rows, pl.ds(pl.multiple_of((i % 4) * 128, 128), 128)] = whole
        return carry

    lax.fori_loop(0, 8, lines, 0, unroll=4)


def pick_tile(t, fx, wt, sp):
    def row(n):
        return jnp.concatenate([fx[n, pl.ds(2 * t, 1), :], fx[n, pl.ds(2 * t + 1, 1), :]], 1)

    kx = jnp.broadcast_to(row(0), (32, 256)).astype(BF)
    ky = jnp.broadcast_to(row(1), (16, 256)).astype(BF)
    index = subl((32, 256)).astype(F32).astype(BF)
    one, zero = jnp.ones((32, 256), BF), jnp.zeros((16, 256), BF)
    base = jnp.where(kx == index, one, jnp.zeros((32, 256), BF))
    hot = []
    for j in range(16):
        here = ky == jnp.asarray(j, BF)
        hot += [jnp.where(here, base[:16], zero), jnp.where(here, base[16:], zero)]
    hot = jnp.concatenate(hot, 0)
    prod = jnp.dot(wt[...], hot, preferred_element_type=F32).astype(BF)
    high = jnp.broadcast_to(row(5), (16, 256)).astype(BF)
    chosen = [prod[:16], prod[256:272]]
    for n in range(1, 16):
        here = high == jnp.asarray(n, BF)
        for part in range(2):
            at = 256 * part + 16 * n
            chosen[part] = jnp.where(here, prod[at : at + 16], chosen[part])
    line = subl((16, 256)).astype(F32) == row(2)
    re, im = [
        jnp.sum(jnp.where(line, v.astype(F32), 0.0), axis=0, keepdims=True) for v in chosen
    ]
    kind = row(4)
    for n in range(4):
        re = jnp.where(kind == float(n), sp[n : n + 1, :], re)
    return re, im * row(3)


def kernel(
    val_in, cond_ref, ve_ref, ce_ref, plane_ref, col_ref, tz, ty, tx, tw,
    rx, cx,
    val_ref, wide, vf, cf, facs, fac, ix, fx, bs, wt, sp, pv, cb, zs, rz, rf, xs,
    s_val, r_val, s_cond, r_cond, s_pass, s_sib, r_sib, s_fac, r_fac,
    s_vf, r_va, r_vb, r_vy, r_vx,
    s_cb, r_cb, s_cx, r_cx, s_cs, r_cs, s_rz, r_rz, r_rw, s_rx, r_rx,
):
    p = lax.axis_index("val")
    c = lax.axis_index("cond")
    y, zl, x, core = c // 16, (c // 8) % 2, (c // 2) % 4, c % 2
    s = zl * 2 + core
    xy = y * 4 + x
    me = s * 4 + p
    base = y * 16 + x * 2
    at_s = lambda n: base + (n >> 1) * 8 + (n & 1)
    by_s = lambda k: c ^ (((k >> 1) << 3) | (k & 1))
    by_xy = lambda k: c ^ (((k >> 2) << 4) | ((k & 3) << 1))
    twin = p == s
    cond_of = lambda o: (c & 9) | ((o >> 2) << 4) | ((o & 3) << 1)

    def remote(src, dst, send, recv, dp, dc):
        return pltpu.make_async_remote_copy(
            src_ref=src, dst_ref=dst, send_sem=send, recv_sem=recv,
            device_id=(dp, dc), device_id_type=pl.DeviceIdType.MESH,
        )

    def put(here, src, dst, send, recv, dp, dc):
        @pl.when(jnp.logical_not(here))
        def _():
            remote(src, dst, send, recv, dp, dc).start()

        @pl.when(here)
        def _():
            pltpu.make_async_copy(src, dst, recv).start()

    def drain(ref, sem):
        pltpu.make_async_copy(ref, ref, sem).wait()

    def drain_bytes(n, sem):
        drain(bs.at[pl.ds(0, n // 512)], sem)

    barrier = pltpu.get_barrier_semaphore()
    for k in range(1, 16):
        for dev in ((p ^ (k >> 2), by_s(k & 3)), (p, by_xy(k))):
            pl.semaphore_signal(
                barrier, inc=1, device_id=dev, device_id_type=pl.DeviceIdType.MESH
            )
    gap = jnp.full((8, 128), ce_ref[0], F32) - jnp.full((8, 128), ve_ref[0], F32)
    facs[...] = jnp.sqrt((1.0 / gap) * (1.0 / (math.sqrt(256.0) * GRID)))
    for i in range(32):
        wide[i : i + 1, :] = val_in[0:1, 128 * i : 128 * i + 128].astype(F32)
    val_ref[...] = wide[...].astype(BF)
    pl.semaphore_wait(barrier, 30)

    half = lambda h: pl.ds(pl.multiple_of(h * 256, 256), 256)
    mine = vf.at[y, zl, x, core]
    put(twin, val_ref, mine, s_val.at[0], r_val, p, at_s(p))
    for k in range(1, 4):
        remote(val_ref, mine, s_val.at[1], r_val, p ^ k, at_s(p)).start()
    put(twin, facs, fac, s_fac, r_fac, s, at_s(p))
    gone = (s - p) & 3
    near = jnp.where(zl == 0, gone >> 1, 1 - (((gone + 1) >> 1) & 1))
    for h in range(2):
        put(
            twin & (core == h), cond_ref.at[half(h)], cf.at[p, half(h)],
            s_cond.at[h], r_cond.at[p], s, at_s(near * 2 + h),
        )

    drain(vf.at[y, :, x], r_val)
    for k in range(1, 4):
        remote(vf.at[y, 0, x], vf.at[y, 0, x], s_vf, r_va, p, by_xy(k)).start()
        remote(vf.at[y, 1, x], vf.at[y, 1, x], s_vf, r_vb, p, by_xy(4 * k)).start()
    drain_bytes(3 * 16384, r_va)
    for k in range(1, 4):
        remote(vf.at[y, 0], vf.at[y, 0], s_vf, r_vy.at[y], p, by_xy(4 * k)).start()
    drain_bytes(3 * 16384, r_vb)
    for k in range(1, 4):
        remote(vf.at[:, 1, x], vf.at[:, 1, x], s_vf, r_vx, p, by_xy(k)).start()

    e1 = jnp.where(p < 2, 2 * zl, 1 + 2 * zl)

    def pass_on(k):
        q = (p - e1 - k) & 3
        part = cf.at[q, half(core)]
        drain(part, r_cond.at[q])
        if k < 2:
            remote(part, part, s_pass, r_cond.at[q], p, c ^ 8).start()
        remote(part, part, s_sib, r_sib.at[q], p, by_s(1)).start()

    pass_on(0)
    pass_on(1)
    order_planes(plane_ref, ix)
    compose_columns(plane_ref, col_ref, ix)
    fold_indices(ix, fx)
    pass_on(2)
    pass_on(3)

    def ready(n):
        o0 = y ^ (2 * (n & 1))
        o1 = o0 ^ 1
        h = core ^ (n >> 1)
        later = (n & 1) == 1

        @pl.when((h == 0) & later)
        def _():
            drain(vf.at[o0, 0], r_vy.at[o0])

        @pl.when(h == 0)
        def _():
            drain(vf.at[o1, 0], r_vy.at[o1])

        @pl.when((h == 1) & jnp.logical_not(later))
        def _():
            drain_bytes(3 * 65536, r_vx)

        @pl.when(n >= 2)
        def _():
            drain(cf.at[o0, half(1 - core)], r_sib.at[o0])
            drain(cf.at[o1, half(1 - core)], r_sib.at[o1])

        return (o0, h), (o1, h)

    transform(ready, vf, cf, tz, ty, tw, bs)
    drain(fac, r_fac)
    lines_of(fac, tx, bs, wt, sp)

    def keep(t, at, step):
        re, im = pick_tile(t, fx, wt, sp)
        pv[pl.ds(at, 1), :] = re[:, :128]
        pv[pl.ds(at + 1, 1), :] = re[:, 128:]
        pv[pl.ds(at + step, 1), :] = im[:, :128]
        pv[pl.ds(at + step + 1, 1), :] = im[:, 128:]

    for t in range(8):
        keep(t, (t // 2) * 8 + (t % 2) * 2, 4)

    slot = lambda n, size: pl.ds(pl.multiple_of(n * size, size), size)
    mine_cb = cb.at[slot(core * 4 + p, 8)]
    for k in range(8):
        to = base + (zl ^ (k & 1)) * 8 + zl
        src = pv.at[slot(p ^ (k >> 1), 8)]
        if k == 0:
            put(core == zl, src, mine_cb, s_cb.at[0], r_cb, p, to)
        else:
            remote(src, mine_cb, s_cb.at[1], r_cb, p ^ (k >> 1), to).start()

    def columns():
        drain(cb, r_cb)
        own = [(-cb[pl.ds(n, 16, stride=4), :]).astype(BF) for n in range(4)]
        cx[pl.ds(xy, 1), pl.ds(core, 1)] = jnp.concatenate(own, 1)[None, None]
        for k in range(1, 16):
            remote(cx.at[xy, core], cx.at[xy, core], s_cx, r_cx, p, by_xy(k)).start()

    def swap_columns():
        drain_bytes(15 * 16384, r_cx)
        remote(cx.at[:, core], cx.at[:, core], s_cs, r_cs, p, by_s(1)).start()

    def send_rows(h, whole):
        for j in range(16):
            if whole:
                v = rz[j, 0:80].astype(F32)[40 * h : 40 * h + 40]
            else:
                v = rz[j, 48 * h : 48 * h + 48].astype(F32)[:40]
            rf[40 * j : 40 * j + 40, :] = v
        low = lanes((32, 128)) < 64
        for m in range(4):
            a = [rf[pl.ds(5 * m + n, 32, stride=20), :] for n in range(5)]
            b = [pltpu.roll(v, 64, 1) for v in a[2:]]
            odd = [jnp.where(low, b[0], b[1]), jnp.where(low, b[1], b[2]), b[2]]
            xs[8 * h + 2 * m] = jnp.concatenate(a[:3], 1).astype(BF)
            xs[8 * h + 2 * m + 1] = jnp.concatenate(odd, 1).astype(BF)
        for k in range(8):
            o = 8 * h + (k ^ (xy & 7))

            @pl.when(o != xy)
            def _():
                remote(xs.at[o], rx.at[xy], s_rx, r_rx, p, cond_of(o)).start()

            @pl.when(o == xy)
            def _():
                rx[pl.ds(xy, 1)] = xs[pl.ds(xy, 1)]

    def rows_to(g, src, dst, recv):
        put(g == s, src, dst, s_rz, recv, p, at_s(g))
        for j in range(1, 4):
            remote(src, dst, s_rz, recv, p ^ j, at_s(g)).start()

    swap = lambda n: ((n & 1) << 1) | (n >> 1)

    def pick(b, carry):
        k, w = b // 2, b % 2
        g = swap(k)
        for e in range(10):
            keep(8 + g * 20 + w * 10 + e, 32 + w * 40 + 2 * e, 20)

        @pl.when(b == 3)
        def _():
            columns()

        @pl.when((w == 1) & (k < 3))
        def _():
            zs[pl.ds(k, 1), 0:80] = pv[32:112, :].astype(BF)[None]
            rows_to(g, zs.at[k, 0:80], rz.at[me, 0:80], r_rz)

        @pl.when(b == 6)
        def _():
            zs[3, 0:48] = pv[32:80, :].astype(BF)
            rows_to(3, zs.at[3, 0:48], rz.at[me, 0:48], r_rz)

        @pl.when(b == 7)
        def _():
            zs[3, 48:96] = pv[72:120, :].astype(BF)
            rows_to(3, zs.at[3, 48:96], rz.at[me, 48:96], r_rw)

        @pl.when((w == 1) & (k == swap(s) + 2))
        def _():
            drain(rz.at[:, 0:80], r_rz)
            send_rows(0, True)
            send_rows(1, True)

        return carry

    lax.fori_loop(0, 8, pick, 0)

    @pl.when((s & 1) == 0)
    def _():
        swap_columns()

    @pl.when(s == 1)
    def _():
        drain(rz.at[:, 0:80], r_rz)
        send_rows(0, True)
        send_rows(1, True)

    @pl.when(s == 3)
    def _():
        drain(rz.at[:, 0:48], r_rz)
        send_rows(0, False)
        drain(rz.at[:, 48:96], r_rw)
        send_rows(1, False)

    @pl.when((s & 1) == 1)
    def _():
        swap_columns()

    drain_bytes(3 * 8192, s_val.at[1])
    for h in range(2):

        @pl.when(jnp.logical_not(twin & (core == h)))
        def _():
            drain(cond_ref.at[half(h)], s_cond.at[h])

    @pl.when(jnp.logical_not(twin))
    def _():
        drain(val_ref, s_val.at[0])
        drain(facs, s_fac)

    drain_bytes(2 * 65536, s_pass)

    drain_bytes(4 * 65536, s_sib)
    drain_bytes(6 * 16384 + 6 * 65536, s_vf)
    drain_bytes(7 * 4096, s_cb.at[1])

    @pl.when(core != zl)
    def _():
        drain_bytes(4096, s_cb.at[0])

    drain_bytes(15 * 16384, s_cx)
    drain(cx.at[:, core], s_cs)

    @pl.when(s < 3)
    def _():
        drain_bytes(316 * 1024, s_rz)

    @pl.when(s == 3)
    def _():
        drain_bytes(312 * 1024, s_rz)

    drain(cx.at[:, 1 - core], r_cs)
    drain_bytes(15 * 24576, r_rx)
    drain_bytes(15 * 24576, s_rx)


def on_device(val_orbitals, cond_orbitals, val_energy, cond_energy, plane_index, column_index):
    vmem = pl.BlockSpec(memory_space=pltpu.VMEM)
    smem = pl.BlockSpec(memory_space=pltpu.SMEM)
    dma = lambda *n: pltpu.SemaphoreType.DMA(n) if n else pltpu.SemaphoreType.DMA
    rx, cx = pl.pallas_call(
        kernel,
        out_shape=(
            jax.ShapeDtypeStruct((16, 32, 384), BF),
            jax.ShapeDtypeStruct((16, 2, 16, 512), BF),
        ),
        in_specs=[vmem, vmem, smem, smem] + [vmem] * 6,
        out_specs=(vmem, vmem),
        scratch_shapes=[
            pltpu.VMEM((32, 128), BF),
            pltpu.VMEM((32, 128), F32),
            pltpu.VMEM((4, 2, 4, 2, 32, 128), BF),
            pltpu.VMEM((4, 512, 128), BF),
            pltpu.VMEM((8, 128), F32),
            pltpu.VMEM((8, 128), F32),
            pltpu.VMEM((176, 128), jnp.int32),
            pltpu.VMEM((6, 176, 128), F32),
            pltpu.VMEM((4096, 128), F32),
            pltpu.VMEM((512, 512), BF),
            pltpu.VMEM((8, 256), F32),
            pltpu.VMEM((128, 128), F32),
            pltpu.VMEM((64, 128), F32),
            pltpu.VMEM((4, 96, 128), BF),
            pltpu.VMEM((16, 96, 128), BF),
            pltpu.VMEM((1280, 128), F32),
            pltpu.VMEM((16, 32, 384), BF),
            dma(2), dma(), dma(2), dma(4), dma(), dma(), dma(4), dma(), dma(),
            dma(), dma(), dma(), dma(4), dma(),
            dma(2), dma(), dma(), dma(), dma(), dma(), dma(), dma(), dma(), dma(), dma(),
        ],
        compiler_params=pltpu.CompilerParams(
            collective_id=0, has_side_effects=True, vmem_limit_bytes=48 * 2**20
        ),
        name="polarizability",
    )(
        val_orbitals,
        cond_orbitals.reshape(512, 128),
        val_energy,
        cond_energy,
        plane_index.reshape(156, 128),
        column_index.reshape(16, 128),
        *[jnp.asarray(t) for t in tables()],
    )
    return lax.dot_general(
        rx.reshape(512, 384)[:, :ROWS], cx.reshape(512, 512), (((0,), (0,)), ((), ())),
        preferred_element_type=F32,
    )


def solution(mesh):
    placed = (P("val", "cond"), P("cond", "val"), P("val"), P("cond"), P(), P())
    return jax.shard_map(
        on_device, mesh=mesh, in_specs=placed, out_specs=P("cond", "val"), check_vma=False
    )
```

```python
import math

import jax
import jax.numpy as jnp
import ml_dtypes
import numpy as np
from jax import lax
from jax.experimental import pallas as pl
from jax.experimental.pallas import tpu as pltpu
from jax.sharding import PartitionSpec as P

N = 64
GRID = N**3
BF = jnp.bfloat16
F32 = jnp.float32
ROWS = 312


def split(a):
    hi = a.astype(ml_dtypes.bfloat16)
    return hi, (a - hi.astype(np.float64)).astype(ml_dtypes.bfloat16)


def tables():
    k = np.arange(N)
    ang = 2 * np.pi * (k[:, None] * k[None, :] % N) / N
    cos, sin = np.cos(ang), np.sin(ang)
    tz = np.zeros((2, N, 2, 2, N))
    for par in range(2):
        tz[par, :, 0, par, :] = cos
        tz[par, :, 1, par, :] = -sin
    tz = tz.reshape(128, 256)
    tz = np.concatenate([tz, tz], 0).astype(ml_dtypes.bfloat16)
    h = np.arange(32)
    ang = 2 * np.pi * (h[:, None] * h[None, :] % 32) / 32
    ty = np.block([[np.cos(ang), np.sin(ang)], [-np.sin(ang), np.cos(ang)]])
    hi, lo = split(ty)
    ty = np.concatenate([hi, lo, hi], 1)
    tx = np.zeros((80, 128))
    tx[:32, :64], tx[:32, 64:] = cos[:32], sin[:32]
    tx[32:64, :64], tx[32:64, 64:] = -sin[:32], cos[:32]
    tx[64, :64] = cos[32]
    tx[65, 64:] = cos[32]
    tx = np.concatenate([tx, tx], 1).astype(ml_dtypes.bfloat16)
    tw = np.zeros((2, 32, 128), np.float32)
    tw[0, :, :64] = 1.0
    ang = 2 * np.pi * h / N
    tw[0, :, 64:] = np.cos(ang)[:, None]
    tw[1, :, 64:] = -np.sin(ang)[:, None]
    return tz, ty, tx, tw


def cond_id(s, xy):
    return (xy // 4) * 16 + (s // 2) * 8 + (xy % 4) * 2 + s % 2


def lanes(shape):
    return lax.broadcasted_iota(jnp.int32, shape, len(shape) - 1)


def subl(shape):
    return lax.broadcasted_iota(jnp.int32, shape, len(shape) - 2)


def order_planes(plane_ref, ix_ref):
    lane = lanes((3, 128))

    def take(start):
        row, off = start // 128, start % 128
        a = plane_ref[row : row + 3, :]
        if off:
            if row + 4 <= 156:
                b = plane_ref[row + 1 : row + 4, :]
            else:
                b = jnp.concatenate([plane_ref[row + 1 : row + 3, :], a[2:3]], 0)
            a = jnp.where(lane < 128 - off, pltpu.roll(a, 128 - off, 1), pltpu.roll(b, 128 - off, 1))
        return a

    for s in range(4):
        for m in range(8):
            even = take(ROWS * cond_id(s, 2 * m))
            odd = take(ROWS * cond_id(s, 2 * m + 1) - 64)
            at = 16 + s * 40 + m * 5
            ix_ref[at : at + 2, :] = even[:2]
            ix_ref[at + 2 : at + 3, :] = jnp.where(lane[:1] < 64, even[2:], odd[:1])
            ix_ref[at + 3 : at + 5, :] = odd[1:]


def compose_columns(plane_ref, col_ref, ix_ref):
    plane = jnp.concatenate([plane_ref[...], jnp.zeros((100, 128), jnp.int32)], 0)
    digits = [
        jnp.transpose(((plane >> sh) & 63).astype(F32), (1, 0)).astype(BF) for sh in (12, 6, 0)
    ]
    left = jnp.concatenate(digits, 0)

    def tile(t, carry):
        col = jnp.concatenate([col_ref[pl.ds(2 * t, 1), :], col_ref[pl.ds(2 * t + 1, 1), :]], 1)
        hot = jnp.where(subl((256, 256)) == (col >> 7), 1.0, 0.0).astype(BF)
        prod = jnp.dot(left, hot, preferred_element_type=F32)
        mask = subl((128, 256)) == (col & 127)
        kx, ky, kz = [
            jnp.sum(jnp.where(mask, prod[128 * d : 128 * d + 128], 0.0), axis=0, keepdims=True)
            for d in range(3)
        ]
        flat = (kx * 4096.0 + ky * 64.0 + kz).astype(jnp.int32)
        ix_ref[pl.ds(2 * t, 1), :] = flat[:, :128]
        ix_ref[pl.ds(2 * t + 1, 1), :] = flat[:, 128:]
        return carry

    lax.fori_loop(0, 8, tile, 0, unroll=8)


def fold_indices(ix_ref, fx_ref):
    n = ix_ref[...]
    kx, ky, kz = n >> 12, (n >> 6) & 63, n & 63
    low = (kx & 31) == 0
    yline = (ky & 31) == 0
    zpoint = (kz & 31) == 0
    neg = kx > 32
    neg = neg | (low & ~yline & ((kx == 0) == (ky > 32)))
    neg = neg | (low & yline & ~zpoint & ((ky == 0) == (kz > 32)))
    special = low & yline & zpoint & ((ky == 0) == (kz == 32))
    turn = lambda k: jnp.where(neg, (64 - k) & 63, k)
    kx, ky, kz = turn(kx), turn(ky), turn(kz)
    slot_y = jnp.where(low & yline, kx, ky)
    fx_ref[0] = (kx & 31).astype(F32)
    fx_ref[1] = jnp.where(special, 99, slot_y & 15).astype(F32)
    line = ((slot_y >> 4) & 1) * 128 + (slot_y >> 5) * 64 + kz
    fx_ref[2] = (line & 15).astype(F32)
    fx_ref[5] = (line >> 4).astype(F32)
    fx_ref[3] = jnp.where(neg, -1.0, 1.0)
    fx_ref[4] = jnp.where(special, (kx >> 5) * 2 + (ky >> 5), 9).astype(F32)


def transform(ready, vf, cf, tz, ty, tw, bs):
    low = lanes((32, 128)) < 64

    def planes(n, carry):
        for y, zl in ready(n):
            a = vf[y, zl].reshape(256, 128).astype(F32)
            b = cf[y, pl.ds(pl.multiple_of(zl * 256, 256), 256), :].astype(F32)
            d = a * b
            hi = d.astype(BF)
            lo = (d - hi.astype(F32)).astype(BF)
            az = jnp.dot(jnp.concatenate([hi, lo], 1), tz[...], preferred_element_type=F32)
            for m in range(4):
                cols = []
                for x in (2 * m, 2 * m + 1):
                    blk = az[x * 32 : x * 32 + 32]
                    cols.append(jnp.concatenate([blk[:, :128], blk[:, 128:]], 0))
                r = jnp.concatenate(cols, 1)
                hi = r.astype(BF)
                lo = (r - hi.astype(F32)).astype(BF)
                g = jnp.dot(ty[...], jnp.concatenate([hi, hi, lo], 0), preferred_element_type=F32)
                for e in range(2):
                    gr, gi = g[:32, e * 128 : e * 128 + 128], g[32:, e * 128 : e * 128 + 128]
                    yr = gr * tw[0] - gi * tw[1]
                    yi = gr * tw[1] + gi * tw[0]
                    at = (y * 16 + zl * 8 + 2 * m + e) * 32
                    for part, v in ((0, yr), (1, yi)):
                        rv = pltpu.roll(v, 64, 1)
                        out = jnp.where(low, rv + v, rv - v)
                        bs[pl.ds(pl.multiple_of(part * 2048 + at, 32), 32), :] = out
        return carry

    lax.fori_loop(0, 4, planes, 0)


def lines_of(fac_ref, tx, bs, wt, sp):
    fac = fac_ref[0:1, :]

    def lines(i, carry):
        b = [bs[pl.ds(4 * i + j, 128, stride=32), :] for j in range(4)]
        r = jnp.concatenate(b, 1)
        hi = r.astype(BF)
        lo = (r - hi.astype(F32)).astype(BF)
        f = jnp.dot(tx[...], jnp.concatenate([hi, lo], 0), preferred_element_type=F32)
        lane = lanes((1, 128))
        top = subl((32, 128)) == 0
        for part in range(2):
            blocks = []
            for j in range(4):
                main = f[32 * part : 32 * part + 32, 128 * j : 128 * j + 128] * fac
                edge = f[64 + part : 65 + part, 128 * j : 128 * j + 128] * fac
                row = main[0:1]
                new = jnp.where(lane < 64, row, edge)
                if j == 0:
                    first = jnp.where(
                        lane < 32,
                        row,
                        jnp.where(
                            lane < 64,
                            pltpu.roll(row, 64, 1),
                            jnp.where(lane < 96, pltpu.roll(edge, 64, 1), edge),
                        ),
                    )
                    if part == 0:

                        @pl.when(i == 0)
                        def _():
                            for n, (v, at) in enumerate(
                                ((row, 32), (row, 64), (edge, 32), (edge, 64))
                            ):
                                pick = jnp.sum(
                                    jnp.where(lane == at, v, 0.0), axis=1, keepdims=True
                                )
                                pick = pick.astype(BF).astype(F32)
                                sp[n : n + 1, :] = jnp.broadcast_to(pick, (1, 256))

                    new = jnp.where(i == 0, first, new)
                blocks.append(jnp.where(top, jnp.broadcast_to(new, (32, 128)), main))
            whole = jnp.transpose(jnp.concatenate(blocks, 0), (1, 0)).astype(BF)
            rows = pl.ds(pl.multiple_of(256 * part + (i // 4) * 128, 128), 128)
            wt[rows, pl.ds(pl.multiple_of((i % 4) * 128, 128), 128)] = whole
        return carry

    lax.fori_loop(0, 8, lines, 0, unroll=8)


def pick_tile(t, fx, wt, sp):
    def row(n):
        return jnp.concatenate([fx[n, pl.ds(2 * t, 1), :], fx[n, pl.ds(2 * t + 1, 1), :]], 1)

    kx = jnp.broadcast_to(row(0), (32, 256)).astype(BF)
    ky = jnp.broadcast_to(row(1), (16, 256)).astype(BF)
    index = subl((32, 256)).astype(F32).astype(BF)
    one, zero = jnp.ones((32, 256), BF), jnp.zeros((16, 256), BF)
    base = jnp.where(kx == index, one, jnp.zeros((32, 256), BF))
    hot = []
    for j in range(16):
        here = ky == jnp.asarray(j, BF)
        hot += [jnp.where(here, base[:16], zero), jnp.where(here, base[16:], zero)]
    hot = jnp.concatenate(hot, 0)
    prod = jnp.dot(wt[...], hot, preferred_element_type=F32).astype(BF)
    high = jnp.broadcast_to(row(5), (16, 256)).astype(BF)
    chosen = [prod[:16], prod[256:272]]
    for n in range(1, 16):
        here = high == jnp.asarray(n, BF)
        for part in range(2):
            at = 256 * part + 16 * n
            chosen[part] = jnp.where(here, prod[at : at + 16], chosen[part])
    line = subl((16, 256)).astype(F32) == row(2)
    re, im = [
        jnp.sum(jnp.where(line, v.astype(F32), 0.0), axis=0, keepdims=True) for v in chosen
    ]
    kind = row(4)
    for n in range(4):
        re = jnp.where(kind == float(n), sp[n : n + 1, :], re)
    return re, im * row(3)


def kernel(
    val_in, cond_ref, ve_ref, ce_ref, plane_ref, col_ref, tz, ty, tx, tw,
    rx, cx,
    val_ref, wide, vf, cf, facs, fac, ix, fx, bs, wt, sp, pv, cb, zs, rz, rf, xs,
    s_val, r_val, s_cond, r_cond, s_pass, s_sib, r_sib, s_fac, r_fac,
    s_vf, r_va, r_vb, r_vy, r_vx,
    s_cb, r_cb, s_cx, r_cx, s_cs, r_cs, s_rz, r_rz, r_rw, s_rx, r_rx,
):
    p = lax.axis_index("val")
    c = lax.axis_index("cond")
    y, zl, x, core = c // 16, (c // 8) % 2, (c // 2) % 4, c % 2
    s = zl * 2 + core
    xy = y * 4 + x
    me = s * 4 + p
    base = y * 16 + x * 2
    at_s = lambda n: base + (n >> 1) * 8 + (n & 1)
    by_s = lambda k: c ^ (((k >> 1) << 3) | (k & 1))
    by_xy = lambda k: c ^ (((k >> 2) << 4) | ((k & 3) << 1))
    twin = p == s
    cond_of = lambda o: (c & 9) | ((o >> 2) << 4) | ((o & 3) << 1)

    def remote(src, dst, send, recv, dp, dc):
        return pltpu.make_async_remote_copy(
            src_ref=src, dst_ref=dst, send_sem=send, recv_sem=recv,
            device_id=(dp, dc), device_id_type=pl.DeviceIdType.MESH,
        )

    def put(here, src, dst, send, recv, dp, dc):
        @pl.when(jnp.logical_not(here))
        def _():
            remote(src, dst, send, recv, dp, dc).start()

        @pl.when(here)
        def _():
            pltpu.make_async_copy(src, dst, recv).start()

    def drain(ref, sem):
        pltpu.make_async_copy(ref, ref, sem).wait()

    def drain_bytes(n, sem):
        drain(bs.at[pl.ds(0, n // 512)], sem)

    barrier = pltpu.get_barrier_semaphore()
    for k in range(1, 16):
        for dev in ((p ^ (k >> 2), by_s(k & 3)), (p, by_xy(k))):
            pl.semaphore_signal(
                barrier, inc=1, device_id=dev, device_id_type=pl.DeviceIdType.MESH
            )
    gap = jnp.full((8, 128), ce_ref[0], F32) - jnp.full((8, 128), ve_ref[0], F32)
    facs[...] = jnp.sqrt((1.0 / gap) * (1.0 / (math.sqrt(256.0) * GRID)))
    for i in range(32):
        wide[i : i + 1, :] = val_in[0:1, 128 * i : 128 * i + 128].astype(F32)
    val_ref[...] = wide[...].astype(BF)
    pl.semaphore_wait(barrier, 30)

    half = lambda h: pl.ds(pl.multiple_of(h * 256, 256), 256)
    mine = vf.at[y, zl, x, core]
    put(twin, val_ref, mine, s_val.at[0], r_val, p, at_s(p))
    for k in range(1, 4):
        remote(val_ref, mine, s_val.at[1], r_val, p ^ k, at_s(p)).start()
    put(twin, facs, fac, s_fac, r_fac, s, at_s(p))
    gone = (s - p) & 3
    near = jnp.where(zl == 0, gone >> 1, 1 - (((gone + 1) >> 1) & 1))
    for h in range(2):
        put(
            twin & (core == h), cond_ref.at[half(h)], cf.at[p, half(h)],
            s_cond.at[h], r_cond.at[p], s, at_s(near * 2 + h),
        )

    order_planes(plane_ref, ix)
    drain(vf.at[y, :, x], r_val)
    for k in range(1, 4):
        remote(vf.at[y, 0, x], vf.at[y, 0, x], s_vf, r_va, p, by_xy(k)).start()
        remote(vf.at[y, 1, x], vf.at[y, 1, x], s_vf, r_vb, p, by_xy(4 * k)).start()
    drain_bytes(3 * 16384, r_va)
    for k in range(1, 4):
        remote(vf.at[y, 0], vf.at[y, 0], s_vf, r_vy.at[y], p, by_xy(4 * k)).start()
    drain_bytes(3 * 16384, r_vb)
    for k in range(1, 4):
        remote(vf.at[:, 1, x], vf.at[:, 1, x], s_vf, r_vx, p, by_xy(k)).start()

    e1 = jnp.where(p < 2, 2 * zl, 1 + 2 * zl)

    def pass_on(k):
        q = (p - e1 - k) & 3
        part = cf.at[q, half(core)]
        drain(part, r_cond.at[q])
        if k < 2:
            remote(part, part, s_pass, r_cond.at[q], p, c ^ 8).start()
        remote(part, part, s_sib, r_sib.at[q], p, by_s(1)).start()

    pass_on(0)
    pass_on(1)
    compose_columns(plane_ref, col_ref, ix)
    fold_indices(ix, fx)
    pass_on(2)
    pass_on(3)

    def ready(n):
        o0 = y ^ (2 * (n & 1))
        o1 = o0 ^ 1
        h = core ^ (n >> 1)
        later = (n & 1) == 1

        @pl.when((h == 0) & later)
        def _():
            drain(vf.at[o0, 0], r_vy.at[o0])

        @pl.when(h == 0)
        def _():
            drain(vf.at[o1, 0], r_vy.at[o1])

        @pl.when((h == 1) & jnp.logical_not(later))
        def _():
            drain_bytes(3 * 65536, r_vx)

        @pl.when(n >= 2)
        def _():
            drain(cf.at[o0, half(1 - core)], r_sib.at[o0])
            drain(cf.at[o1, half(1 - core)], r_sib.at[o1])

        return (o0, h), (o1, h)

    transform(ready, vf, cf, tz, ty, tw, bs)
    drain(fac, r_fac)
    lines_of(fac, tx, bs, wt, sp)

    def keep(t, at, step):
        re, im = pick_tile(t, fx, wt, sp)
        pv[pl.ds(at, 1), :] = re[:, :128]
        pv[pl.ds(at + 1, 1), :] = re[:, 128:]
        pv[pl.ds(at + step, 1), :] = im[:, :128]
        pv[pl.ds(at + step + 1, 1), :] = im[:, 128:]

    for t in range(8):
        keep(t, (t // 2) * 8 + (t % 2) * 2, 4)

    slot = lambda n, size: pl.ds(pl.multiple_of(n * size, size), size)
    mine_cb = cb.at[slot(core * 4 + p, 8)]
    for k in range(8):
        to = base + (zl ^ (k & 1)) * 8 + zl
        src = pv.at[slot(p ^ (k >> 1), 8)]
        if k == 0:
            put(core == zl, src, mine_cb, s_cb.at[0], r_cb, p, to)
        else:
            remote(src, mine_cb, s_cb.at[1], r_cb, p ^ (k >> 1), to).start()

    def columns():
        drain(cb, r_cb)
        own = [(-cb[pl.ds(n, 16, stride=4), :]).astype(BF) for n in range(4)]
        cx[pl.ds(xy, 1), pl.ds(core, 1)] = jnp.concatenate(own, 1)[None, None]
        for k in range(1, 16):
            remote(cx.at[xy, core], cx.at[xy, core], s_cx, r_cx, p, by_xy(k)).start()

    def swap_columns():
        drain_bytes(15 * 16384, r_cx)
        remote(cx.at[:, core], cx.at[:, core], s_cs, r_cs, p, by_s(1)).start()

    def send_rows(h, whole):
        for j in range(16):
            if whole:
                v = rz[j, 0:80].astype(F32)[40 * h : 40 * h + 40]
            else:
                v = rz[j, 48 * h : 48 * h + 48].astype(F32)[:40]
            rf[40 * j : 40 * j + 40, :] = v
        low = lanes((32, 128)) < 64
        for m in range(4):
            a = [rf[pl.ds(5 * m + n, 32, stride=20), :] for n in range(5)]
            b = [pltpu.roll(v, 64, 1) for v in a[2:]]
            odd = [jnp.where(low, b[0], b[1]), jnp.where(low, b[1], b[2]), b[2]]
            xs[8 * h + 2 * m] = jnp.concatenate(a[:3], 1).astype(BF)
            xs[8 * h + 2 * m + 1] = jnp.concatenate(odd, 1).astype(BF)
        for k in range(8):
            o = 8 * h + (k ^ (xy & 7))

            @pl.when(o != xy)
            def _():
                remote(xs.at[o], rx.at[xy], s_rx, r_rx, p, cond_of(o)).start()

            @pl.when(o == xy)
            def _():
                rx[pl.ds(xy, 1)] = xs[pl.ds(xy, 1)]

    def rows_to(g, src, dst, recv):
        put(g == s, src, dst, s_rz, recv, p, at_s(g))
        for j in range(1, 4):
            remote(src, dst, s_rz, recv, p ^ j, at_s(g)).start()

    swap = lambda n: ((n & 1) << 1) | (n >> 1)

    def pick(b, carry):
        k, w = b // 2, b % 2
        g = swap(k)
        for e in range(10):
            keep(8 + g * 20 + w * 10 + e, 32 + w * 40 + 2 * e, 20)

        @pl.when(b == 3)
        def _():
            columns()

        @pl.when((w == 1) & (k < 3))
        def _():
            zs[pl.ds(k, 1), 0:80] = pv[32:112, :].astype(BF)[None]
            rows_to(g, zs.at[k, 0:80], rz.at[me, 0:80], r_rz)

        @pl.when(b == 6)
        def _():
            zs[3, 0:48] = pv[32:80, :].astype(BF)
            rows_to(3, zs.at[3, 0:48], rz.at[me, 0:48], r_rz)

        @pl.when(b == 7)
        def _():
            zs[3, 48:96] = pv[72:120, :].astype(BF)
            rows_to(3, zs.at[3, 48:96], rz.at[me, 48:96], r_rw)

        @pl.when((w == 1) & (k == swap(s) + 2))
        def _():
            drain(rz.at[:, 0:80], r_rz)
            send_rows(0, True)
            send_rows(1, True)

        return carry

    lax.fori_loop(0, 8, pick, 0)

    swap_columns()

    @pl.when(s == 1)
    def _():
        drain(rz.at[:, 0:80], r_rz)
        send_rows(0, True)
        send_rows(1, True)

    @pl.when(s == 3)
    def _():
        drain(rz.at[:, 0:48], r_rz)
        send_rows(0, False)
        drain(rz.at[:, 48:96], r_rw)
        send_rows(1, False)

    drain_bytes(3 * 8192, s_val.at[1])
    for h in range(2):

        @pl.when(jnp.logical_not(twin & (core == h)))
        def _():
            drain(cond_ref.at[half(h)], s_cond.at[h])

    @pl.when(jnp.logical_not(twin))
    def _():
        drain(val_ref, s_val.at[0])
        drain(facs, s_fac)

    drain_bytes(2 * 65536, s_pass)

    drain_bytes(4 * 65536, s_sib)
    drain_bytes(6 * 16384 + 6 * 65536, s_vf)
    drain_bytes(7 * 4096, s_cb.at[1])

    @pl.when(core != zl)
    def _():
        drain_bytes(4096, s_cb.at[0])

    drain_bytes(15 * 16384, s_cx)
    drain(cx.at[:, core], s_cs)

    @pl.when(s < 3)
    def _():
        drain_bytes(316 * 1024, s_rz)

    @pl.when(s == 3)
    def _():
        drain_bytes(312 * 1024, s_rz)

    drain(cx.at[:, 1 - core], r_cs)
    drain_bytes(15 * 24576, r_rx)
    drain_bytes(15 * 24576, s_rx)


def on_device(val_orbitals, cond_orbitals, val_energy, cond_energy, plane_index, column_index):
    vmem = pl.BlockSpec(memory_space=pltpu.VMEM)
    smem = pl.BlockSpec(memory_space=pltpu.SMEM)
    dma = lambda *n: pltpu.SemaphoreType.DMA(n) if n else pltpu.SemaphoreType.DMA
    rx, cx = pl.pallas_call(
        kernel,
        out_shape=(
            jax.ShapeDtypeStruct((16, 32, 384), BF),
            jax.ShapeDtypeStruct((16, 2, 16, 512), BF),
        ),
        in_specs=[vmem, vmem, smem, smem] + [vmem] * 6,
        out_specs=(vmem, vmem),
        scratch_shapes=[
            pltpu.VMEM((32, 128), BF),
            pltpu.VMEM((32, 128), F32),
            pltpu.VMEM((4, 2, 4, 2, 32, 128), BF),
            pltpu.VMEM((4, 512, 128), BF),
            pltpu.VMEM((8, 128), F32),
            pltpu.VMEM((8, 128), F32),
            pltpu.VMEM((176, 128), jnp.int32),
            pltpu.VMEM((6, 176, 128), F32),
            pltpu.VMEM((4096, 128), F32),
            pltpu.VMEM((512, 512), BF),
            pltpu.VMEM((8, 256), F32),
            pltpu.VMEM((128, 128), F32),
            pltpu.VMEM((64, 128), F32),
            pltpu.VMEM((4, 96, 128), BF),
            pltpu.VMEM((16, 96, 128), BF),
            pltpu.VMEM((1280, 128), F32),
            pltpu.VMEM((16, 32, 384), BF),
            dma(2), dma(), dma(2), dma(4), dma(), dma(), dma(4), dma(), dma(),
            dma(), dma(), dma(), dma(4), dma(),
            dma(2), dma(), dma(), dma(), dma(), dma(), dma(), dma(), dma(), dma(), dma(),
        ],
        compiler_params=pltpu.CompilerParams(
            collective_id=0, has_side_effects=True, vmem_limit_bytes=48 * 2**20
        ),
        name="polarizability",
    )(
        val_orbitals,
        cond_orbitals.reshape(512, 128),
        val_energy,
        cond_energy,
        plane_index.reshape(156, 128),
        column_index.reshape(16, 128),
        *[jnp.asarray(t) for t in tables()],
    )
    return lax.dot_general(
        rx.reshape(512, 384)[:, :ROWS], cx.reshape(512, 512), (((0,), (0,)), ((), ())),
        preferred_element_type=F32,
    )


def solution(mesh):
    placed = (P("val", "cond"), P("cond", "val"), P("val"), P("cond"), P(), P())
    return jax.shard_map(
        on_device, mesh=mesh, in_specs=placed, out_specs=P("cond", "val"), check_vma=False
    )
```
